128 devices in a mesh: rep: 4 (over z_hi, core), fsdp: 32 (over z_lo, y, x).
Axes of the slice: x: 4, y: 4, z: 4 (z_hi: 2, z_lo: 2; z = z_hi * 2 + z_lo), core: 2. Of those that a mesh axis runs over, the one named last changes fastest.
Arguments:
- params: float32 [8192, 1024], P('fsdp'), may hold values from -6 to 6
- momentum: float32 [8192, 1024], P('fsdp'), may hold values from -6 to 6
- local_params: bfloat16 [4, 8192, 1024], P('rep', 'fsdp'), may hold values from -6 to 6
- exps: int32 [4], replicated, may hold values from 6 to 9
- inputs: bfloat16 [131072, 8192], P(('rep', 'fsdp')), may hold values from -24 to 24
- key_cotangent: bfloat16 [131072, 1024], P(('rep', 'fsdp')), may hold values from -0.03125 to 0.03125
Outputs:
- new_params: float32 [8192, 1024], P('fsdp')
- new_momentum: float32 [8192, 1024], P('fsdp')
- kv_grad: float32 [4, 8192, 1024], P('rep', 'fsdp')
The draws below stay inside these ranges and needn't reach their ends.
All inputs are finite; a program needn't handle non-finite values.
Results may differ from the reference program's by a relative error of at most 0.0075.
Values sent between devices are 32-bit elements; how exact they have to be, the bound alone decides.
No kernel may reach another device: no remote copies, remote signals or barrier semaphores. Data moves between devices by JAX's collectives and lax.ppermute only.
A program may use at most 128 MiB of HBM per device.

```python
import jax
import jax.numpy as jnp
from jax import lax

D = 8192
TOK_DEV = 1024
KD = 1024
TOKENS = 32768
N_REP = 4
N_FSDP = 32


def place_ends(values, stream_key, low, top_value):
    spot = [jax.random.randint(jax.random.fold_in(stream_key, axis), (), 0, length) for axis, length in enumerate(values.shape)]
    longest = values.shape.index(max(values.shape))
    next_to = spot[:longest] + [(spot[longest] + 1) % values.shape[longest]] + spot[longest + 1:]
    return values.at[tuple(spot)].set(low).at[tuple(next_to)].set(top_value)


def with_spikes(result, rng, source, target, shards_of, factor):
    def block_of(axis_at):
        return (jnp.arange(result.shape[axis_at]) // (result.shape[axis_at] // shards_of)).reshape((-1,) + (1,) * (result.ndim - 1 - axis_at))

    one_side = jax.random.permutation(rng, shards_of)[block_of(target)]
    second = (block_of(target) + shards_of // 2) % shards_of
    return jnp.where((block_of(source) == one_side) | (block_of(source) == second), factor * result, result)


def shard_levels(stream_key, dims, pieces, least, top_value):
    level, own = 1.0, jax.random.fold_in(stream_key, 6)
    for dim, shards_of in pieces:
        steps = jnp.exp(jax.random.uniform(jax.random.fold_in(own, dim), (shards_of,), jnp.float32, least / len(pieces), top_value / len(pieces)))
        level = level * jnp.repeat(steps, dims[dim] // shards_of).reshape([-1 if axis == dim else 1 for axis in range(len(dims))])
    return level


def gaussian(stream_key, shape, spread, limit, pieces=(), held_as=jnp.bfloat16):
    drawn = spread * jax.random.normal(stream_key, shape, jnp.float32)
    if pieces:
        drawn = drawn * shard_levels(stream_key, shape, pieces, -0.22, 0.18)
    return jnp.clip(drawn, -limit, limit).astype(held_as)


def noise_with(rng, shape, scale, reach, pieces, heavy, dtype=jnp.bfloat16):
    array = scale * jax.random.normal(rng, shape, jnp.float32)
    if pieces:
        array = array * shard_levels(rng, shape, pieces, -0.22, 0.18)
    return jnp.clip(with_spikes(array, jax.random.fold_in(rng, 3), *heavy), -reach, reach).astype(dtype)


def setup_inputs(seed: int = 0) -> dict:
    splits = jax.random.split(jax.random.key(seed), 7)
    params = gaussian(splits[0], (D, KD), 1.0, 6.0, ((0, 32),), jnp.float32)
    momentum = gaussian(splits[1], (D, KD), 0.5, 6.0, ((0, 32),), jnp.float32)
    local_params = gaussian(splits[2], (N_REP, D, KD), 1.0, 6.0, ((0, 4), (1, 32)))
    exps = place_ends(jax.random.randint(splits[3], (N_REP,), 6, 10), jax.random.fold_in(splits[3], 1), 6, 9).astype(jnp.int32)
    inputs = noise_with(splits[4], (N_REP * TOKENS, D), 1.0, 24.0, ((0, 128),), (0, 1, 128, 5.5))
    key_cotangent = gaussian(splits[5], (N_REP * TOKENS, KD), TOKENS ** -0.5, 0.03125, ((0, 128),))
    return dict(params=params, momentum=momentum, local_params=local_params, exps=exps, inputs=inputs, key_cotangent=key_cotangent)


def reference(params, momentum, local_params, exps, inputs, key_cotangent):
    up = jnp.exp2(exps.astype(jnp.float32))[:, None, None]
    delta = params[None] - local_params.astype(jnp.float32)
    coded = jnp.clip(delta * up, -448.0, 448.0).astype(jnp.bfloat16)
    outer_grad = lax.optimization_barrier(jnp.sum(coded.astype(jnp.float32) / up, axis=0)) / N_REP
    new_momentum = 0.9 * momentum + outer_grad
    new_params = params - 0.7 * (outer_grad + 0.9 * new_momentum)
    blocks_x = inputs.reshape(N_REP, N_FSDP, TOK_DEV, D)
    blocks_k = key_cotangent.reshape(N_REP, N_FSDP, TOK_DEV, KD)

    def group_grad(pair):

        def step(total, item):
            rows_x, rows_k = item
            part = jnp.dot(rows_x.T, rows_k, preferred_element_type=jnp.float32)
            return (total + part, None)
        total, _ = lax.scan(step, jnp.zeros((D, KD), jnp.float32), pair)
        return total
    kv_grad = lax.map(group_grad, (blocks_x, blocks_k))
    return (new_params, new_momentum, kv_grad)
```

```python
import jax
import jax.numpy as jnp
from jax import lax
from jax.experimental import pallas as pl
from jax.experimental.pallas import tpu as pltpu
from jax.sharding import PartitionSpec as P

AXES = {"z": (16, 2), "y": (4, 4), "x": (1, 4)}

CHUNKS = (
    (176, "xyz", 1),
    (176, "xyz", -1),
    (176, "yxz", 1),
    (176, "yxz", -1),
    (80, "zxy", 1),
    (80, "zxy", -1),
    (80, "zyx", 1),
    (80, "zyx", -1),
)


def shift(axis, step):
    stride, size = AXES[axis]
    pairs = []
    for source in range(32):
        place = source // stride % size
        pairs.append((source, source + ((place + step) % size - place) * stride))
    return pairs


def send(array, axis, step):
    return lax.ppermute(array, "fsdp", shift(axis, step))


def blocks_of(fixed, free):
    out = []
    for dz in range(2) if "z" in free else [fixed["z"]]:
        for dy in range(4) if "y" in free else [fixed["y"]]:
            for dx in range(4) if "x" in free else [fixed["x"]]:
                out.append((dz, dy, dx))
    return out


class Piece:
    def __init__(self, chunk, blocks, terms):
        self.chunk, self.blocks, self.terms = chunk, blocks, terms


def multiply(inputs, keys, ids, segments):
    width = 256
    depth = inputs.shape[0]
    total = sum(len(seg[0].blocks) for seg in segments)
    rows, operands, in_specs, out_specs, out_shape, plan = [], [], [], [], [], []
    order = [b for seg in segments for b in seg[0].blocks]
    rows.append(ids(order))

    def spec(rows_n, row):
        return pl.BlockSpec((1, rows_n, width), lambda i, table, row=row: (table[row, i], 0, 0))

    start = 0
    flops = 0
    moved = total * depth * width * 2
    for seg in segments:
        count = len(seg[0].blocks)
        for piece in seg:
            key = keys[piece.chunk]
            height = key.shape[0]
            entry = [start, count, len(operands), len(piece.terms)]
            operands.append(key)
            in_specs.append(pl.BlockSpec((height, depth), lambda i, table: (0, 0)))
            for array, places in piece.terms:
                row = [places[piece.blocks[min(max(i - start, 0), count - 1)]] for i in range(total)]
                rows.append(jnp.array(row, jnp.int32))
                operands.append(array)
                in_specs.append(spec(height, len(rows) - 1))
            rows.append(jnp.array([min(max(i - start, 0), count - 1) for i in range(total)], jnp.int32))
            out_specs.append(spec(height, len(rows) - 1))
            out_shape.append(jax.ShapeDtypeStruct((count, height, width), jnp.float32))
            plan.append(entry)
            flops += 2 * count * height * width * depth
            moved += (1 + len(piece.terms)) * count * height * width * 4 + height * depth * 2
        start += count
    n_in = len(operands)

    def body(table, x_ref, *refs):
        ins, outs = refs[:n_in], refs[n_in:]
        step = pl.program_id(0)
        for (first, count, at, terms), out in zip(plan, outs):

            @pl.when((step >= first) & (step < first + count))
            def _(at=at, terms=terms, out=out):
                value = jnp.dot(ins[at][...], x_ref[...], preferred_element_type=jnp.float32)
                for term in range(terms):
                    value = value + ins[at + 1 + term][0]
                out[0] = value

    return pl.pallas_call(
        body,
        grid_spec=pltpu.PrefetchScalarGridSpec(
            num_scalar_prefetch=1,
            grid=(total,),
            in_specs=[pl.BlockSpec((depth, width), lambda i, table: (0, table[0, i]))] + in_specs,
            out_specs=out_specs,
        ),
        out_shape=out_shape,
        compiler_params=pltpu.CompilerParams(
            dimension_semantics=("arbitrary",), vmem_limit_bytes=40 * 1024 * 1024
        ),
        cost_estimate=pl.CostEstimate(flops=flops, bytes_accessed=moved, transcendentals=0),
    )(jnp.stack(rows), inputs, *operands)


def gradient(inputs, cotangent):
    me = lax.axis_index("fsdp")
    mine = (me // 16, me // 4 % 4, me % 4)

    def ids(order):
        at = jnp.array(order, jnp.int32)
        return (
            16 * ((mine[0] + at[:, 0]) % 2) + 4 * ((mine[1] + at[:, 1]) % 4) + (mine[2] + at[:, 2]) % 4
        ).astype(jnp.int32)

    keys, low = [], 0
    for height, _, _ in CHUNKS:
        keys.append(cotangent[:, low : low + height].T)
        low += height

    arrived = [[] for _ in CHUNKS]

    def piece(chunk, blocks):
        terms = []
        for array, places in arrived[chunk]:
            if all(b in places for b in blocks):
                terms.append((array, places))
            else:
                assert not any(b in places for b in blocks)
        return Piece(chunk, blocks, terms)

    def run(segments):
        return multiply(inputs, keys, ids, segments)

    def land(chunk, array, blocks, axis, step):
        at = "zyx".index(axis)
        places = {}
        for n, b in enumerate(blocks):
            moved = list(b)
            moved[at] = (moved[at] - step) % AXES[axis][1]
            places[tuple(moved)] = n
        arrived[chunk].append((send(array, axis, step), places))

    def selected(chunk, stage, offset):
        order = CHUNKS[chunk][1]
        fixed = {a: 0 for a in order[:stage]}
        fixed[order[stage]] = offset
        return blocks_of(fixed, order[stage + 1 :])

    def far(pair, stage):
        axis = CHUNKS[pair[0]][1][stage]
        if axis == "z":
            todo = [(c, 1, 1) for c in pair]
        else:
            todo = [(c, 2, CHUNKS[c][2]) for c in pair]
        blocks = selected(pair[0], stage, todo[0][1])
        for (c, _, step), array in zip(todo, run([[piece(c, blocks) for c in pair]])):
            land(c, array, blocks, axis, step)

    def near(pair, stage, turn):
        axis = CHUNKS[pair[0]][1][stage]
        if axis == "z":
            return
        segments, todo = [], []
        for c in pair:
            step = turn * CHUNKS[c][2]
            blocks = selected(c, stage, step % 4)
            segments.append([piece(c, blocks)])
            todo.append((c, blocks, step))
        for (c, blocks, step), array in zip(todo, run(segments)):
            land(c, array, blocks, axis, step)

    pairs = ((0, 1), (2, 3), (4, 5), (6, 7))
    for stage in range(3):
        for pair in pairs:
            far(pair, stage)
        for turn in (-1, 1):
            for pair in pairs:
                near(pair, stage, turn)
    own = [(0, 0, 0)]
    parts = []
    for pair in pairs:
        parts += run([[piece(c, own) for c in pair]])
    return jnp.concatenate([p[0] for p in parts], axis=0).T


def outer(params, momentum, local_params, exps):
    groups = lax.axis_size("rep")
    group = lax.axis_index("rep")
    picked = jnp.sum(jnp.where(jnp.arange(groups) == group, exps, 0))
    scale_up = jnp.left_shift(1, picked).astype(jnp.float32)
    delta = params - local_params[0].astype(jnp.float32)
    coded = jnp.clip(delta * scale_up, -448.0, 448.0).astype(jnp.bfloat16)
    decoded = coded.astype(jnp.float32) / scale_up
    core = group % 2
    half = decoded.shape[0] // 2
    kept = lax.dynamic_slice_in_dim(decoded, core * half, half, 0)
    given = lax.dynamic_slice_in_dim(decoded, (1 - core) * half, half, 0)
    other_core = [(r, r ^ 1) for r in range(4)]
    other_chip = [(r, r ^ 2) for r in range(4)]
    kept = kept + lax.ppermute(given, "rep", other_core)
    kept = kept + lax.ppermute(kept, "rep", other_chip)
    rest = lax.ppermute(kept, "rep", other_core)
    first = core == 0
    total = jnp.concatenate([jnp.where(first, kept, rest), jnp.where(first, rest, kept)], axis=0)
    outer_grad = total / groups
    fresh = 0.9 * momentum + outer_grad
    return params - 0.7 * (outer_grad + 0.9 * fresh), fresh


def local(params, momentum, local_params, exps, inputs, key_cotangent):
    new_params, new_momentum = outer(params, momentum, local_params, exps)
    kv_grad = gradient(inputs, key_cotangent)
    return (new_params, new_momentum, kv_grad[None])


def solution(mesh):
    in_specs = (
        P("fsdp", None),
        P("fsdp", None),
        P("rep", "fsdp", None),
        P(),
        P(("rep", "fsdp"), None),
        P(("rep", "fsdp"), None),
    )
    out_specs = (P("fsdp", None), P("fsdp", None), P("rep", "fsdp", None))
    return jax.shard_map(local, mesh=mesh, in_specs=in_specs, out_specs=out_specs, check_vma=False)
```

```python
import jax
import jax.numpy as jnp
from jax import lax
from jax.experimental import pallas as pl
from jax.experimental.pallas import tpu as pltpu
from jax.sharding import PartitionSpec as P

WIDTH = 256
ROW = 4
A = 224
B = 160
C = 128
X_RINGS = [[16 * z + 4 * y + x for x in range(4)] for z in range(2) for y in range(4)]

LONG = pl.CostEstimate(flops=10**11, bytes_accessed=10**8, transcendentals=0)


def multiply(inputs, keys, place, strips, wanted, swapped=False, after=()):
    depth = inputs.shape[0]
    span = ROW * WIDTH
    halves = 2

    def body(table, *refs):
        xs, ks, outs = refs[:halves], refs[halves : halves + len(keys)], refs[len(refs) - len(wanted) :]
        step = pl.program_id(0)
        part = depth // halves

        def emit(key, out):
            value = jnp.dot(ks[key][:, :part], xs[0][...], preferred_element_type=jnp.float32)
            value += jnp.dot(ks[key][:, part:], xs[1][...], preferred_element_type=jnp.float32)
            for x in range(ROW):
                piece = value[:, x * WIDTH : (x + 1) * WIDTH]
                if swapped:
                    out[x, 0] = piece
                else:
                    out[0, x] = piece

        for (key, first, count), out in zip(wanted, outs):
            if count == len(strips):
                emit(key, out)
            else:
                pl.when((step >= first) & (step < first + count))(lambda key=key, out=out: emit(key, out))

    def out_spec(key, first, count):
        rows = keys[key].shape[0]

        def at(i, table):
            n = jnp.clip(i - first, 0, count - 1)
            return (0, n, 0, 0) if swapped else (n, 0, 0, 0)

        return pl.BlockSpec((ROW, 1, rows, WIDTH) if swapped else (1, ROW, rows, WIDTH), at)

    shapes = [
        (ROW, n, keys[k].shape[0], WIDTH) if swapped else (n, ROW, keys[k].shape[0], WIDTH) for k, _, n in wanted
    ]
    table = 4 * ((place[0] + jnp.array([s[0] for s in strips])) % 2) + (
        place[1] + jnp.array([s[1] for s in strips])
    ) % 4
    return pl.pallas_call(
        body,
        grid_spec=pltpu.PrefetchScalarGridSpec(
            num_scalar_prefetch=1,
            grid=(len(strips),),
            in_specs=[
                pl.BlockSpec((depth // halves, span), lambda i, table, s=s: (s, table[i])) for s in range(halves)
            ]
            + [pl.BlockSpec(k.shape, lambda i, table: (0, 0)) for k in keys]
            + [pl.BlockSpec(memory_space=pl.ANY) for _ in after],
            out_specs=[out_spec(*w) for w in wanted],
        ),
        out_shape=[jax.ShapeDtypeStruct(s, jnp.float32) for s in shapes],
        compiler_params=pltpu.CompilerParams(
            dimension_semantics=("arbitrary",), vmem_limit_bytes=60 * 1024 * 1024
        ),
        cost_estimate=LONG,
    )(table.astype(jnp.int32), *[inputs] * halves, *keys, *after)


def along_y(array, step):
    return lax.ppermute(
        array, "fsdp", [(f, f // 16 * 16 + (f // 4 + step) % 4 * 4 + f % 4) for f in range(32)]
    )


def along_z(array):
    return lax.ppermute(array, "fsdp", [(f, (f + 16) % 32) for f in range(32)])


def over_x(array):
    return lax.psum_scatter(array, "fsdp", scatter_dimension=0, axis_index_groups=X_RINGS, tiled=True)[0]


def combine(body, arrays, shapes, after=()):
    def kernel(*refs):
        body(*refs[: len(arrays)], *refs[len(arrays) + len(after) :])

    return pl.pallas_call(
        kernel,
        in_specs=[pl.BlockSpec(memory_space=pltpu.VMEM)] * len(arrays)
        + [pl.BlockSpec(memory_space=pl.ANY)] * len(after),
        out_specs=[pl.BlockSpec(memory_space=pltpu.VMEM)] * len(shapes),
        out_shape=[jax.ShapeDtypeStruct(s, jnp.float32) for s in shapes],
        compiler_params=pltpu.CompilerParams(vmem_limit_bytes=60 * 1024 * 1024),
        cost_estimate=LONG,
    )(*arrays, *after)


def reduce_a(array, after):
    half = A // 2

    def part(ref, z, y, h):
        return ref[4 * z + y, h * half : (h + 1) * half, :]

    def first(a, up, down):
        for z in range(2):
            up[0, z], up[1, z] = part(a, z, 2, 0), part(a, z, 1, 1)
            down[0, z], down[1, z] = part(a, z, 2, 1), part(a, z, 3, 0)

    up, down = combine(first, [array], [(2, 2, half, WIDTH)] * 2, after)
    up_in, down_in = along_y(up, 1), along_y(down, -1)
    after = yield [up]

    def second(a, up_in, down_in, up, down):
        for z in range(2):
            up[z] = part(a, z, 1, 0) + up_in[0, z]
            down[z] = part(a, z, 3, 1) + down_in[0, z]

    up, down = combine(second, [array, up_in, down_in], [(2, half, WIDTH)] * 2, after)
    up_last, down_last = along_y(up, 1), along_y(down, -1)
    after = yield [up]

    def third(a, up_in, down_in, up_last, down_last, keep, cross):
        for z, out in enumerate((keep, cross)):
            out[:half, :] = part(a, z, 0, 0) + down_in[1, z] + up_last[z]
            out[half:, :] = part(a, z, 0, 1) + up_in[1, z] + down_last[z]

    keep, cross = combine(third, [array, up_in, down_in, up_last, down_last], [(A, WIDTH)] * 2, after)
    yield keep, along_z(cross), [keep]


def reduce_c(near, far, after):
    def part(refs, x, y, h):
        return refs[h][y, x] + refs[2][y, x, h * C : (h + 1) * C, :]

    def first(n0, n1, f, up, down):
        refs = (n0, n1, f)
        for x in range(ROW):
            up[0, x], up[1, x] = part(refs, x, 2, 0), part(refs, x, 1, 1)
            down[0, x], down[1, x] = part(refs, x, 2, 1), part(refs, x, 3, 0)

    up, down = combine(first, [*near, far], [(2, ROW, C, WIDTH)] * 2, after)
    up_in, down_in = along_y(up, 1), along_y(down, -1)
    after = yield [up]

    def second(n0, n1, f, up_in, down_in, up, down):
        refs = (n0, n1, f)
        for x in range(ROW):
            up[x] = part(refs, x, 1, 0) + up_in[0, x]
            down[x] = part(refs, x, 3, 1) + down_in[0, x]

    up, down = combine(second, [*near, far, up_in, down_in], [(ROW, C, WIDTH)] * 2, after)
    up_last, down_last = along_y(up, 1), along_y(down, -1)
    after = yield [up]

    def third(n0, n1, f, up_in, down_in, up_last, down_last, out):
        refs = (n0, n1, f)
        for x in range(ROW):
            out[x, :C, :] = part(refs, x, 0, 0) + down_in[1, x] + up_last[x]
            out[x, C:, :] = part(refs, x, 0, 1) + up_in[1, x] + down_last[x]

    (own,) = combine(
        third, [*near, far, up_in, down_in, up_last, down_last], [(ROW, 2 * C, WIDTH)], after
    )
    yield over_x(own), [own]


def local(params, momentum, local_params, exps, inputs, cotangent):
    groups = lax.axis_size("rep")
    group = lax.axis_index("rep")
    picked = jnp.sum(jnp.where(jnp.arange(groups) == group, exps, 0))
    scale_up = jnp.left_shift(1, picked).astype(jnp.float32)
    delta = params - local_params[0].astype(jnp.float32)
    coded = jnp.clip(delta * scale_up, -448.0, 448.0).astype(jnp.bfloat16)
    decoded = coded.astype(jnp.float32) / scale_up
    total = lax.psum(decoded, "rep")

    me = lax.axis_index("fsdp")
    place = (me // 16, me // 4 % 4)
    keys, low = [], 0
    for height in (A, A, B, B, C, C):
        keys.append(cotangent[:, low : low + height].T)
        low += height
    whole = [(z, y) for z in range(2) for y in range(4)]

    def run(*args, **kwargs):
        return multiply(inputs, *args[:1], place, *args[1:], **kwargs)

    (a1,) = run(keys[0:1], whole, [(0, 0, 8)], swapped=True, after=[decoded])
    a1_x = over_x(a1)
    b_far = run(keys[2:4], [(0, 2), (1, 2)], [(0, 0, 2), (1, 0, 2)], after=[a1])
    b_up1, b_down1 = along_y(b_far[0], 1), along_y(b_far[1], -1)
    (c_far,) = run(
        [jnp.concatenate(keys[4:6])], [(1, y) for y in range(4)], [(0, 0, 4)], after=b_far[:1]
    )
    c_z = along_z(c_far)
    (a2,) = run(keys[1:2], whole, [(0, 0, 8)], swapped=True, after=[c_far])
    a2_x = over_x(a2)
    rest = run(
        keys[2:6],
        [(1, 0), (0, 0), (0, 1), (0, 2), (0, 3)],
        [(0, 0, 2), (1, 0, 2), (2, 1, 4), (3, 1, 4)],
        after=[a2],
    )
    b_own, c_near = rest[:2], rest[2:]
    b_near = run(
        keys[2:4],
        [(0, 1), (1, 1), (0, 3), (1, 3)],
        [(0, 0, 2), (1, 0, 2), (0, 2, 2), (1, 2, 2)],
        after=rest[:1],
    )
    b_up2, b_down2 = along_y(b_near[1], 1), along_y(b_near[2], -1)

    def b_third(near0, near3, up1, down1, up, down):
        for z in range(2):
            for x in range(ROW):
                up[z, x] = near0[z, x] + up1[z, x]
                down[z, x] = near3[z, x] + down1[z, x]

    b_last = combine(
        b_third, [b_near[0], b_near[3], b_up1, b_down1], [(2, ROW, B, WIDTH)] * 2
    )
    b_up3, b_down3 = along_y(b_last[0], 1), along_y(b_last[1], -1)

    def nesterov(weights, moment, total, new_weights, fresh):
        outer_grad = total[...] / groups
        fresh[...] = 0.9 * moment[...] + outer_grad
        new_weights[...] = weights[...] - 0.7 * (outer_grad + 0.9 * fresh[...])

    new_params, new_momentum = combine(
        nesterov, [params, momentum, total], [params.shape] * 2, b_last[:1]
    )

    ring_1 = reduce_a(a1_x[:, :, :], [new_params])
    done = next(ring_1)

    def b_home(own0, own1, up2, down2, up3, down3, out):
        for z in range(2):
            for x in range(ROW):
                low = 2 * B * z
                out[x, low : low + B, :] = own0[1 - z, x] + down2[z, x] + up3[z, x]
                out[x, low + B : low + 2 * B, :] = own1[1 - z, x] + up2[z, x] + down3[z, x]

    (b_sum,) = combine(
        b_home, [*b_own, b_up2, b_down2, b_up3, b_down3], [(ROW, 4 * B, WIDTH)], done
    )
    b_x = over_x(b_sum)
    ring_c = reduce_c(c_near, c_z, [b_sum])
    done = next(ring_c)
    done = ring_1.send(done)
    done = ring_c.send(done)
    a1_keep, a1_in, done = ring_1.send(done)
    c_own, done = ring_c.send(done)
    ring_2 = reduce_a(a2_x, done)
    done = next(ring_2)
    done = ring_2.send(done)
    a2_keep, a2_in, done = ring_2.send(done)
    b_in = along_z(b_x[2 * B :])
    kv_grad = jnp.concatenate([a1_keep + a1_in, a2_keep + a2_in, b_x[: 2 * B] + b_in, c_own], axis=0).T
    return (new_params, new_momentum, kv_grad[None])


def solution(mesh):
    in_specs = (
        P("fsdp", None),
        P("fsdp", None),
        P("rep", "fsdp", None),
        P(),
        P(("rep", "fsdp"), None),
        P(("rep", "fsdp"), None),
    )
    out_specs = (P("fsdp", None), P("fsdp", None), P("rep", "fsdp", None))
    return jax.shard_map(local, mesh=mesh, in_specs=in_specs, out_specs=out_specs, check_vma=False)
```

```python
import jax
import jax.numpy as jnp
from jax import lax
from jax.experimental import pallas as pl
from jax.experimental.pallas import tpu as pltpu
from jax.sharding import PartitionSpec as P

WIDTH = 256
ROW = 4
STRIP = ROW * WIDTH
STRIPS = 8
A = 416
B = 352
C = 256
X_RINGS = [[16 * z + 4 * y + x for x in range(4)] for z in range(2) for y in range(4)]
COST = pl.CostEstimate(flops=10**10, bytes_accessed=10**7, transcendentals=0)
MIB = 1024 * 1024


def store_blocks(value, out, swapped):
    for x in range(ROW):
        piece = value[:, x * WIDTH : (x + 1) * WIDTH]
        if swapped:
            out[x, 0] = piece
        else:
            out[0, x] = piece


def first_products(inputs, cotangent, place):
    depth, columns = cotangent.shape
    halves = 2
    part = depth // halves

    def body(table, *refs):
        xs, k, out, strips, turned = refs[:halves], *refs[halves:]
        step = pl.program_id(0)

        @pl.when(step == 0)
        def _():
            turned[...] = k[...].T

        value = jnp.dot(turned[:A, :part], xs[0][...], preferred_element_type=jnp.float32)
        value += jnp.dot(turned[:A, part:], xs[1][...], preferred_element_type=jnp.float32)
        store_blocks(value, out, True)
        for s in range(halves):
            strips[step, s * part : (s + 1) * part, :] = xs[s][...]

    at = jnp.arange(STRIPS)
    table = 4 * ((place[0] + at // 4) % 2) + (place[1] + at % 4) % 4
    out, strips, turned = pl.pallas_call(
        body,
        grid_spec=pltpu.PrefetchScalarGridSpec(
            num_scalar_prefetch=1,
            grid=(STRIPS,),
            in_specs=[pl.BlockSpec((part, STRIP), lambda i, table, s=s: (s, table[i])) for s in range(halves)]
            + [pl.BlockSpec((depth, columns), lambda i, table: (0, 0), pipeline_mode=pl.Buffered(1))],
            out_specs=[
                pl.BlockSpec((ROW, 1, A, WIDTH), lambda i, table: (0, i, 0, 0)),
                pl.BlockSpec(memory_space=pltpu.VMEM),
                pl.BlockSpec(memory_space=pltpu.VMEM),
            ],
        ),
        out_shape=[
            jax.ShapeDtypeStruct((ROW, STRIPS, A, WIDTH), jnp.float32),
            pltpu.VMEM((STRIPS, depth, STRIP), inputs.dtype),
            pltpu.VMEM((columns, depth), cotangent.dtype),
        ],
        compiler_params=pltpu.CompilerParams(dimension_semantics=("arbitrary",), vmem_limit_bytes=40 * MIB),
        cost_estimate=COST,
    )(table.astype(jnp.int32), *[inputs] * halves, cotangent)
    return out, pltpu.with_memory_space_constraint(strips, pltpu.VMEM), pltpu.with_memory_space_constraint(
        turned, pltpu.VMEM
    )


def products(strips, turned, count, strip_of, wanted, after):
    def body(x, k, *refs):
        outs = refs[len(after) :]
        step = pl.program_id(0)
        for (low, height, first, number), out in zip(wanted, outs):

            def emit(low=low, height=height, out=out):
                value = jnp.dot(
                    k[low : low + height, :], x[strip_of(step)], preferred_element_type=jnp.float32
                )
                store_blocks(value, out, False)

            if number == count:
                emit()
            else:
                pl.when((step >= first) & (step < first + number))(emit)

    def out_spec(low, height, first, number):
        return pl.BlockSpec(
            (1, ROW, height, WIDTH), lambda i: (jnp.clip(i - first, 0, number - 1), 0, 0, 0)
        )

    return pl.pallas_call(
        body,
        grid=(count,),
        in_specs=[pl.BlockSpec(memory_space=pltpu.VMEM)] * 2 + [pl.BlockSpec(memory_space=pl.ANY)] * len(after),
        out_specs=[out_spec(*w) for w in wanted],
        out_shape=[jax.ShapeDtypeStruct((n, ROW, height, WIDTH), jnp.float32) for _, height, _, n in wanted],
        compiler_params=pltpu.CompilerParams(dimension_semantics=("arbitrary",), vmem_limit_bytes=40 * MIB),
        cost_estimate=COST,
    )(strips, turned, *after)


def combine(body, pieces, shapes, after=()):
    pieces = [p if isinstance(p, tuple) else (p, p.shape, (0,) * p.ndim) for p in pieces]

    def kernel(*refs):
        body(*refs[: len(pieces)], *refs[len(pieces) + len(after) :])

    return pl.pallas_call(
        kernel,
        grid=(1,),
        in_specs=[pl.BlockSpec(block, lambda i, at=at: at) for _, block, at in pieces]
        + [pl.BlockSpec(memory_space=pl.ANY)] * len(after),
        out_specs=[pl.BlockSpec(s, lambda i, at=(0,) * len(s): at) for s in shapes],
        out_shape=[jax.ShapeDtypeStruct(s, jnp.float32) for s in shapes],
        compiler_params=pltpu.CompilerParams(vmem_limit_bytes=60 * MIB),
        cost_estimate=COST,
    )(*[p[0] for p in pieces], *after)


def along_y(array, step):
    return lax.ppermute(
        array, "fsdp", [(f, f // 16 * 16 + (f // 4 + step) % 4 * 4 + f % 4) for f in range(32)]
    )


def along_z(array):
    return lax.ppermute(array, "fsdp", [(f, (f + 16) % 32) for f in range(32)])


def over_x(array):
    return lax.psum_scatter(array, "fsdp", scatter_dimension=0, axis_index_groups=X_RINGS, tiled=True)[0]


def reduce_y(terms, outer, rows, home):
    shape = (outer, rows, WIDTH)
    count = len(terms(0, 0))

    def total(refs):
        value = refs[0][...].reshape(shape)
        for ref in refs[1:]:
            value = value + ref[...].reshape(shape)
        return value

    def first(*refs):
        *groups, up, down = [refs[i * count : (i + 1) * count] for i in range(4)] + list(refs[4 * count :])
        up[0], up[1], down[0], down[1] = [total(g) for g in groups]

    after = yield
    pieces = terms(2, 0) + terms(1, 1) + terms(2, 1) + terms(3, 0)
    up, down = combine(first, pieces, [(2,) + shape] * 2, after)
    up_in, down_in = along_y(up, 1), along_y(down, -1)
    after = yield [up]

    def got(array, n):
        return (array, (1,) + shape, (n, 0, 0, 0))

    def second(*refs):
        refs[-2][...] = total(refs[: count + 1])
        refs[-1][...] = total(refs[count + 1 : -2])

    up, down = combine(
        second, terms(1, 0) + [got(up_in, 0)] + terms(3, 1) + [got(down_in, 0)], [shape] * 2, after
    )
    up_last, down_last = along_y(up, 1), along_y(down, -1)
    after = yield [up]
    shapes, write = home

    def third(*refs):
        n = count + 2
        write(total(refs[:n]), total(refs[n : 2 * n]), *refs[2 * n :])

    pieces = terms(0, 0) + [got(down_in, 1), up_last] + terms(0, 1) + [got(up_in, 1), down_last]
    out = combine(third, pieces, shapes, after)
    yield out


def local(params, momentum, local_params, exps, inputs, cotangent):
    groups = lax.axis_size("rep")
    group = lax.axis_index("rep")
    me = lax.axis_index("fsdp")

    a, strips, turned = first_products(inputs, cotangent, (me // 16, me // 4 % 4))
    a_x = over_x(a).reshape(2, 4, A, WIDTH)
    half = B // 2
    b_low, b_high, c_low = A, A + half, A + B
    b_far = products(
        strips, turned, 2, lambda i: 2 + 4 * i, [(b_low, half, 0, 2), (b_high, half, 0, 2)], [a]
    )
    b_up1, b_down1 = along_y(b_far[0], 1), along_y(b_far[1], -1)
    (c_far,) = products(strips, turned, 4, lambda i: 4 + i, [(c_low, C, 0, 4)], b_far[:1])
    c_z = along_z(c_far)
    b_near = products(
        strips,
        turned,
        4,
        lambda i: 1 + 4 * lax.rem(i, 2) + 2 * (i // 2),
        [(low, half, first, 2) for first in (0, 2) for low in (b_low, b_high)],
        [c_far],
    )
    b_up2, b_down2 = along_y(b_near[1], 1), along_y(b_near[2], -1)
    *b_own, c_near = products(
        strips,
        turned,
        5,
        lambda i: jnp.where(i == 0, 4, i - 1),
        [(b_low, half, 0, 2), (b_high, half, 0, 2), (c_low, C, 1, 4)],
        b_near[:1],
    )

    picked = jnp.sum(jnp.where(jnp.arange(groups) == group, exps, 0))
    scale_up = jnp.full((8, 128), jnp.left_shift(1, picked).astype(jnp.float32))

    def copy(scale, out):
        out[...] = scale[...]

    (scale_late,) = combine(copy, [scale_up], [scale_up.shape], [c_near])
    scale = scale_late[0, 0]
    delta = params - local_params[0].astype(jnp.float32)
    coded = jnp.clip(delta * scale, -448.0, 448.0).astype(jnp.bfloat16)
    total = lax.psum(coded.astype(jnp.float32) / scale, "rep")

    def b_third(near_up, near_down, got_up, got_down, up, down):
        up[...] = near_up[...] + got_up[...]
        down[...] = near_down[...] + got_down[...]

    b_last = combine(b_third, [b_near[0], b_near[3], b_up1, b_down1], [(2, ROW, half, WIDTH)] * 2, [scale_late])
    b_up3, b_down3 = along_y(b_last[0], 1), along_y(b_last[1], -1)

    def b_home(own0, own1, up2, down2, up3, down3, out):
        for z in range(2):
            for x in range(ROW):
                low = B * z
                out[x, low : low + half, :] = own0[1 - z, x] + down2[z, x] + up3[z, x]
                out[x, low + half : low + B, :] = own1[1 - z, x] + up2[z, x] + down3[z, x]

    (b_sum,) = combine(b_home, [*b_own, b_up2, b_down2, b_up3, b_down3], [(ROW, 2 * B, WIDTH)])
    b_x = over_x(b_sum)

    def nesterov(weights, moment, total, new_weights, fresh):
        outer_grad = total[...] / groups
        fresh[...] = 0.9 * moment[...] + outer_grad
        new_weights[...] = weights[...] - 0.7 * (outer_grad + 0.9 * fresh[...])

    def a_terms(dy, h):
        return [(a_x, (2, 1, A // 2, WIDTH), (0, dy, h, 0))]

    def a_home(low, high, keep, cross):
        keep[: A // 2, :], keep[A // 2 :, :] = low[0], high[0]
        cross[: A // 2, :], cross[A // 2 :, :] = low[1], high[1]

    def c_terms(dy, h):
        block = (1, ROW, C // 2, WIDTH)
        return [(c_near, block, (dy, 0, h, 0)), (c_z, block, (dy, 0, h, 0))]

    def c_home(low, high, out):
        out[:, : C // 2, :], out[:, C // 2 :, :] = low, high

    ring_a = reduce_y(a_terms, 2, A // 2, ([(A, WIDTH)] * 2, a_home))
    ring_c = reduce_y(c_terms, ROW, C // 2, ([(ROW, C, WIDTH)], c_home))
    next(ring_a), next(ring_c)
    done = ring_c.send([b_sum])
    done = ring_a.send(done)
    new_params, new_momentum = combine(nesterov, [params, momentum, total], [params.shape] * 2, done)
    done = ring_c.send([new_params])
    done = ring_a.send(done)
    (c_sum,) = ring_c.send(done)
    c_own = over_x(c_sum)
    a_keep, a_cross = ring_a.send([c_sum])
    a_in = along_z(a_cross)
    b_in = along_z(b_x[B:])

    def assemble(keep_a, got_a, keep_b, got_b, own_c, out):
        value = jnp.concatenate([keep_a[...] + got_a[...], keep_b[...] + got_b[...], own_c[...]], axis=0)
        out[0] = value.T

    (kv_grad,) = combine(
        assemble, [a_keep, a_in, (b_x, (B, WIDTH), (0, 0)), b_in, c_own], [(1, WIDTH, A + B + C)]
    )
    return (new_params, new_momentum, kv_grad)


def solution(mesh):
    in_specs = (
        P("fsdp", None),
        P("fsdp", None),
        P("rep", "fsdp", None),
        P(),
        P(("rep", "fsdp"), None),
        P(("rep", "fsdp"), None),
    )
    out_specs = (P("fsdp", None), P("fsdp", None), P("rep", "fsdp", None))
    return jax.shard_map(local, mesh=mesh, in_specs=in_specs, out_specs=out_specs, check_vma=False)
```

```python
import jax
import jax.numpy as jnp
from jax import lax
from jax.experimental import pallas as pl
from jax.experimental.pallas import tpu as pltpu
from jax.sharding import PartitionSpec as P

WIDTH = 256
ROW = 4
STRIP = ROW * WIDTH
STRIPS = 8
A = 416
B = 352
C = 256
X_RINGS = [[16 * z + 4 * y + x for x in range(4)] for z in range(2) for y in range(4)]
LONG = pl.CostEstimate(flops=5 * 10**10, bytes_accessed=1000, transcendentals=0)
SHORT = pl.CostEstimate(flops=5 * 10**9, bytes_accessed=1000, transcendentals=0)
MIB = 1024 * 1024


def far_products(inputs, cotangent, table, wanted):
    depth, columns = cotangent.shape

    def body(table, x, k, *refs):
        *outs, strips, turned = refs
        step = pl.program_id(0)

        @pl.when(step == 0)
        def _():
            turned[...] = k[...].T

        for (low, height), out in zip(wanted, outs):
            value = jnp.dot(turned[low : low + height, :], x[...], preferred_element_type=jnp.float32)
            for place in range(ROW):
                out[0, (place - table[STRIPS]) & (ROW - 1)] = value[:, place * WIDTH : (place + 1) * WIDTH]
        strips[step] = x[...]

    *outs, strips, turned = pl.pallas_call(
        body,
        grid_spec=pltpu.PrefetchScalarGridSpec(
            num_scalar_prefetch=1,
            grid=(2,),
            in_specs=[
                pl.BlockSpec((depth, STRIP), lambda i, table: (0, table[2 + 4 * i])),
                pl.BlockSpec((depth, columns), lambda i, table: (0, 0), pipeline_mode=pl.Buffered(1)),
            ],
            out_specs=[pl.BlockSpec((1, ROW, height, WIDTH), lambda i, table: (i, 0, 0, 0)) for _, height in wanted]
            + [pl.BlockSpec(memory_space=pltpu.VMEM)] * 2,
        ),
        out_shape=[jax.ShapeDtypeStruct((2, ROW, height, WIDTH), jnp.float32) for _, height in wanted]
        + [pltpu.VMEM((2, depth, STRIP), inputs.dtype), pltpu.VMEM((columns, depth), cotangent.dtype)],
        compiler_params=pltpu.CompilerParams(dimension_semantics=("arbitrary",), vmem_limit_bytes=56 * MIB),
        cost_estimate=LONG,
    )(table, inputs, cotangent)
    return (
        outs,
        pltpu.with_memory_space_constraint(strips, pltpu.VMEM),
        pltpu.with_memory_space_constraint(turned, pltpu.VMEM),
    )


def all_products(inputs, strips, turned, table, low, height, after):
    depth = inputs.shape[0]

    def order(i):
        rest = i - 2 + (i >= 4).astype(jnp.int32) + (i >= 7).astype(jnp.int32)
        return jnp.where(i < 2, 2 + 4 * i, rest)

    def body(table, x, held, k, *refs):
        out = refs[-1]
        step = pl.program_id(0)

        def emit(block):
            value = jnp.dot(k[low : low + height, :], block, preferred_element_type=jnp.float32)
            for place in range(ROW):
                out[place, 0] = value[:, place * WIDTH : (place + 1) * WIDTH]

        pl.when(step < 2)(lambda: emit(held[jnp.minimum(step, 1)]))
        pl.when(step >= 2)(lambda: emit(x[...]))

    return pl.pallas_call(
        body,
        grid_spec=pltpu.PrefetchScalarGridSpec(
            num_scalar_prefetch=1,
            grid=(STRIPS,),
            in_specs=[pl.BlockSpec((depth, STRIP), lambda i, table: (0, table[order(jnp.maximum(i, 2))]))]
            + [pl.BlockSpec(memory_space=pltpu.VMEM)] * 2
            + [pl.BlockSpec(memory_space=pl.ANY)] * len(after),
            out_specs=pl.BlockSpec((ROW, 1, height, WIDTH), lambda i, table: (0, order(i), 0, 0)),
        ),
        out_shape=jax.ShapeDtypeStruct((ROW, STRIPS, height, WIDTH), jnp.float32),
        compiler_params=pltpu.CompilerParams(dimension_semantics=("arbitrary",), vmem_limit_bytes=56 * MIB),
        cost_estimate=LONG,
    )(table, inputs, strips, turned, *after)


def products(inputs, turned, table, count, strip_of, wanted, after):
    depth = inputs.shape[0]

    def body(table, x, k, *refs):
        outs = refs[len(after) :]
        step = pl.program_id(0)
        for (low, height, first, number, _), out in zip(wanted, outs):

            def emit(low=low, height=height, out=out):
                value = jnp.dot(k[low : low + height, :], x[...], preferred_element_type=jnp.float32)
                for place in range(ROW):
                    out[0, (place - table[STRIPS]) & (ROW - 1)] = value[:, place * WIDTH : (place + 1) * WIDTH]

            if number == count:
                emit()
            else:
                pl.when((step >= first) & (step < first + number))(emit)

    def out_spec(low, height, first, number, order):
        def at(i, table):
            n = jnp.clip(i - first, 0, number - 1)
            return (n if order > 0 else number - 1 - n, 0, 0, 0)

        return pl.BlockSpec((1, ROW, height, WIDTH), at)

    return pl.pallas_call(
        body,
        grid_spec=pltpu.PrefetchScalarGridSpec(
            num_scalar_prefetch=1,
            grid=(count,),
            in_specs=[
                pl.BlockSpec((depth, STRIP), lambda i, table: (0, table[strip_of(i)])),
                pl.BlockSpec(memory_space=pltpu.VMEM),
            ]
            + [pl.BlockSpec(memory_space=pl.ANY)] * len(after),
            out_specs=[out_spec(*w) for w in wanted],
        ),
        out_shape=[jax.ShapeDtypeStruct((w[3], ROW, w[1], WIDTH), jnp.float32) for w in wanted],
        compiler_params=pltpu.CompilerParams(dimension_semantics=("arbitrary",), vmem_limit_bytes=60 * MIB),
        cost_estimate=LONG,
    )(table, inputs, turned, *after)


def combine(body, pieces, shapes, after=()):
    pieces = [p if isinstance(p, tuple) else (p, p.shape, (0,) * p.ndim) for p in pieces]

    def kernel(*refs):
        body(*refs[: len(pieces)], *refs[len(pieces) + len(after) :])

    return pl.pallas_call(
        kernel,
        grid=(1,),
        in_specs=[pl.BlockSpec(block, lambda i, at=at: at) for _, block, at in pieces]
        + [pl.BlockSpec(memory_space=pl.ANY)] * len(after),
        out_specs=[pl.BlockSpec(s, lambda i, at=(0,) * len(s): at) for s in shapes],
        out_shape=[jax.ShapeDtypeStruct(s, jnp.float32) for s in shapes],
        compiler_params=pltpu.CompilerParams(vmem_limit_bytes=60 * MIB),
        cost_estimate=SHORT,
    )(*[p[0] for p in pieces], *after)


def along(axis, array, step):
    stride = 1 if axis == "x" else 4
    pairs = [(f, f + ((f // stride + step) % 4 - f // stride % 4) * stride) for f in range(32)]
    return lax.ppermute(array, "fsdp", pairs)


def along_z(array):
    return lax.ppermute(array, "fsdp", [(f, (f + 16) % 32) for f in range(32)])


def over_x(array):
    return lax.psum_scatter(array, "fsdp", scatter_dimension=0, axis_index_groups=X_RINGS, tiled=True)[0]


def reduce_ring(axis, terms, outer, rows):
    shape = (outer, rows, WIDTH)
    count = len(terms(0, 0))

    def total(refs):
        value = refs[0][...].reshape(shape)
        for ref in refs[1:]:
            value = value + ref[...].reshape(shape)
        return value

    def first(*refs):
        up, down = refs[4 * count :]
        up[0], up[1], down[0], down[1] = [total(refs[i * count : (i + 1) * count]) for i in range(4)]

    after = yield
    pieces = terms(2, 0) + terms(1, 1) + terms(2, 1) + terms(3, 0)
    up, down = combine(first, pieces, [(2,) + shape] * 2, after)
    up_in, down_in = along(axis, up, 1), along(axis, down, -1)
    after = yield [up]

    def got(array):
        return [(array, (1,) + shape, (0, 0, 0, 0))]

    def second(*refs):
        up, down = refs[-2:]
        up[...], down[...] = total(refs[: count + 1]), total(refs[count + 1 : -2])

    pieces = terms(1, 0) + got(up_in) + terms(3, 1) + got(down_in)
    up, down = combine(second, pieces, [shape] * 2, after)
    up_last, down_last = along(axis, up, 1), along(axis, down, -1)
    yield [up], lambda half: [(down_in, 1), (up_last, None)] if half == 0 else [(up_in, 1), (down_last, None)]


def settle(low, high, write, shapes, after):
    def body(*refs):
        sums = []
        for group, pieces in ((refs[: len(low)], low), (refs[len(low) : len(low) + len(high)], high)):
            shape = [n for n in pieces[-1][1]]
            value = group[0][...].reshape(shape)
            for ref in group[1:]:
                value = value + ref[...].reshape(shape)
            sums.append(value)
        write(*sums, *refs[len(low) + len(high) :])

    return combine(body, low + high, shapes, after)


def local(params, momentum, local_params, exps, inputs, cotangent):
    groups = lax.axis_size("rep")
    group = lax.axis_index("rep")
    me = lax.axis_index("fsdp")
    at = jnp.arange(STRIPS + 1)
    table = 4 * ((me // 16 + at // 4) % 2) + (me // 4 + at) % 4
    table = jnp.where(at == STRIPS, me % 4, table).astype(jnp.int32)

    half = B // 2
    b_low, b_high, c_low = A, A + half, A + B
    b_far, strips, turned = far_products(inputs, cotangent, table, [(b_low, half), (b_high, half)])
    b_up1, b_down1 = along("y", b_far[0], 1), along("y", b_far[1], -1)
    a = all_products(inputs, strips, turned, table, 0, A, b_far[:1])
    a_x = over_x(a).reshape(2, 4, A, WIDTH)
    (c_far,) = products(inputs, turned, table, 4, lambda i: 4 + i, [(c_low, C, 0, 4, 1)], [a])
    c_z = along_z(c_far)
    b_near = products(
        inputs,
        turned,
        table,
        4,
        lambda i: 1 + 4 * lax.rem(i, 2) + 2 * (i // 2),
        [(low, half, first, 2, 1) for first in (0, 2) for low in (b_low, b_high)],
        [c_far],
    )
    b_up2, b_down2 = along("y", b_near[1], 1), along("y", b_near[2], -1)
    *b_own, c_near = products(
        inputs,
        turned,
        table,
        5,
        lambda i: jnp.where(i == 0, 4, i - 1),
        [(b_low, half, 0, 2, -1), (b_high, half, 0, 2, -1), (c_low, C, 1, 4, 1)],
        b_near[:1],
    )

    def b_third(near_up, near_down, got_up, got_down, up, down):
        up[...] = near_up[...] + got_up[...]
        down[...] = near_down[...] + got_down[...]

    b_last = combine(b_third, [b_near[0], b_near[3], b_up1, b_down1], [(2, ROW, half, WIDTH)] * 2, [c_near])
    b_up3, b_down3 = along("y", b_last[0], 1), along("y", b_last[1], -1)

    def b_terms(dx, h):
        arrays = (b_own[0], b_down2, b_up3) if h == 0 else (b_own[1], b_up2, b_down3)
        return [(array, (2, 1, half, WIDTH), (0, dx, 0, 0)) for array in arrays]

    def c_terms(dy, h):
        block = (1, ROW, C // 2, WIDTH)
        return [(c_near, block, (dy, 0, h, 0)), (c_z, block, (dy, 0, h, 0))]

    def a_terms(dy, h):
        return [(a_x, (2, 1, A // 2, WIDTH), (0, dy, h, 0))]

    def whole(arrived):
        return [
            (array, array.shape, (0,) * 3) if n is None else (array, (1,) + array.shape[1:], (n, 0, 0, 0))
            for array, n in arrived
        ]

    ring_b = reduce_ring("x", b_terms, 2, half)
    ring_c = reduce_ring("y", c_terms, ROW, C // 2)
    ring_a = reduce_ring("y", a_terms, 2, A // 2)
    next(ring_b), next(ring_c), next(ring_a)
    done = ring_b.send(b_last[:1])
    done = ring_c.send(done)

    picked = jnp.sum(jnp.where(jnp.arange(groups) == group, exps, 0))
    scale_up = jnp.full((8, 128), jnp.left_shift(1, picked).astype(jnp.float32))

    def copy(scale, out):
        out[...] = scale[...]

    done = combine(copy, [scale_up], [scale_up.shape], done)
    scale = done[0][0, 0]
    delta = params - local_params[0].astype(jnp.float32)
    coded = jnp.clip(delta * scale, -448.0, 448.0).astype(jnp.bfloat16)
    total = lax.psum(coded.astype(jnp.float32) / scale, "rep")

    done, b_got = ring_b.send(done)
    done, c_got = ring_c.send(done)
    done = ring_a.send(done)

    def c_x_terms(dx, h):
        block = (1, 1, C // 2, WIDTH)
        terms = [(c_near, block, (0, dx, h, 0)), (c_z, block, (0, dx, h, 0))]
        for array, n in c_got(h):
            terms.append((array, block[1:], (dx, 0, 0)) if n is None else (array, block, (n, dx, 0, 0)))
        return terms

    def keep_and_cross(low, high, keep, cross):
        rows = low.shape[1]
        keep[:rows, :], keep[rows:, :] = low[0], high[0]
        cross[:rows, :], cross[rows:, :] = low[1], high[1]

    b_keep, b_cross = settle(
        b_terms(0, 0) + whole(b_got(0)), b_terms(0, 1) + whole(b_got(1)), keep_and_cross, [(B, WIDTH)] * 2, done
    )
    b_in = along_z(b_cross)
    ring_cx = reduce_ring("x", c_x_terms, 1, C // 2)
    next(ring_cx)
    done = ring_cx.send([b_keep])
    done, cx_got = ring_cx.send(done)
    done, a_got = ring_a.send(done)

    def c_home(low, high, out):
        out[: C // 2, :], out[C // 2 :, :] = low[0], high[0]

    (c_own,) = settle(
        c_x_terms(0, 0) + whole(cx_got(0)), c_x_terms(0, 1) + whole(cx_got(1)), c_home, [(C, WIDTH)], done
    )
    a_keep, a_cross = settle(
        a_terms(0, 0) + whole(a_got(0)), a_terms(0, 1) + whole(a_got(1)), keep_and_cross, [(A, WIDTH)] * 2, [c_own]
    )
    a_in = along_z(a_cross)

    def nesterov(weights, moment, total, new_weights, fresh):
        outer_grad = total[...] / groups
        fresh[...] = 0.9 * moment[...] + outer_grad
        new_weights[...] = weights[...] - 0.7 * (outer_grad + 0.9 * fresh[...])

    new_params, new_momentum = combine(nesterov, [params, momentum, total], [params.shape] * 2, [a_keep])

    def assemble(keep_a, got_a, keep_b, got_b, own_c, out):
        value = jnp.concatenate([keep_a[...] + got_a[...], keep_b[...] + got_b[...], own_c[...]], axis=0)
        out[0] = value.T

    (kv_grad,) = combine(
        assemble, [a_keep, a_in, b_keep, b_in, c_own], [(1, WIDTH, A + B + C)], [new_params]
    )
    return (new_params, new_momentum, kv_grad)


def solution(mesh):
    in_specs = (
        P("fsdp", None),
        P("fsdp", None),
        P("rep", "fsdp", None),
        P(),
        P(("rep", "fsdp"), None),
        P(("rep", "fsdp"), None),
    )
    out_specs = (P("fsdp", None), P("fsdp", None), P("rep", "fsdp", None))
    return jax.shard_map(local, mesh=mesh, in_specs=in_specs, out_specs=out_specs, check_vma=False)
```

```python
import jax
import jax.numpy as jnp
from jax import lax
from jax.experimental import pallas as pl
from jax.experimental.pallas import tpu as pltpu
from jax.sharding import PartitionSpec as P

WIDTH = 256
ROW = 4
STRIP = ROW * WIDTH
STRIPS = 8
A = 416
B = 352
C = 256
X_RINGS = [[16 * z + 4 * y + x for x in range(4)] for z in range(2) for y in range(4)]
LONG = pl.CostEstimate(flops=2 * 10**10, bytes_accessed=1000, transcendentals=0)
SHORT = pl.CostEstimate(flops=4 * 10**9, bytes_accessed=1000, transcendentals=0)
MIB = 1024 * 1024


def all_products(inputs, cotangent, table, height):
    depth, columns = cotangent.shape

    def body(table, x, k, out, turned):
        step = pl.program_id(0)

        @pl.when(step == 0)
        def _():
            turned[...] = k[...].T

        value = jnp.dot(turned[:height, :], x[...], preferred_element_type=jnp.float32)
        for place in range(ROW):
            out[place, 0] = value[:, place * WIDTH : (place + 1) * WIDTH]

    out, turned = pl.pallas_call(
        body,
        grid_spec=pltpu.PrefetchScalarGridSpec(
            num_scalar_prefetch=1,
            grid=(STRIPS,),
            in_specs=[
                pl.BlockSpec((depth, STRIP), lambda i, table: (0, table[i])),
                pl.BlockSpec((depth, columns), lambda i, table: (0, 0), pipeline_mode=pl.Buffered(1)),
            ],
            out_specs=[
                pl.BlockSpec((ROW, 1, height, WIDTH), lambda i, table: (0, i, 0, 0)),
                pl.BlockSpec(memory_space=pltpu.VMEM),
            ],
        ),
        out_shape=[
            jax.ShapeDtypeStruct((ROW, STRIPS, height, WIDTH), jnp.float32),
            pltpu.VMEM((columns, depth), cotangent.dtype),
        ],
        compiler_params=pltpu.CompilerParams(dimension_semantics=("arbitrary",), vmem_limit_bytes=60 * MIB),
        cost_estimate=LONG,
    )(table, inputs, cotangent)
    return out, pltpu.with_memory_space_constraint(turned, pltpu.VMEM)


def crossing_products(inputs, turned, table, low, half, after):
    depth = inputs.shape[0]

    def body(table, x, k, *refs):
        soon, late = refs[-2:]
        step = pl.program_id(0)

        def emit(h, out, n):
            value = jnp.dot(k[low + h * half : low + (h + 1) * half, :], x[...], preferred_element_type=jnp.float32)
            for place in range(ROW):
                out[n, (place - table[STRIPS]) & (ROW - 1)] = value[:, place * WIDTH : (place + 1) * WIDTH]

        for at, first, second in ((0, soon, soon), (1, late, soon), (2, soon, late), (3, late, late)):

            @pl.when(step == at)
            def _(at=at, first=first, second=second):
                emit(0, first, 1 if at == 2 else 0)
                emit(1, second, 0 if at == 1 else 1)

    block = (2, ROW, half, WIDTH)
    return pl.pallas_call(
        body,
        grid_spec=pltpu.PrefetchScalarGridSpec(
            num_scalar_prefetch=1,
            grid=(4,),
            in_specs=[
                pl.BlockSpec(
                    (depth, STRIP),
                    lambda i, table: (0, table[4 + jnp.where(i == 0, 2, jnp.where(i == 3, 0, 2 * i - 1))]),
                ),
                pl.BlockSpec(memory_space=pltpu.VMEM),
            ]
            + [pl.BlockSpec(memory_space=pl.ANY)] * len(after),
            out_specs=[
                pl.BlockSpec(block, lambda i, table: (jnp.minimum(i, 1), 0, 0, 0)),
                pl.BlockSpec(block, lambda i, table: (i // 3, 0, 0, 0)),
            ],
        ),
        out_shape=[jax.ShapeDtypeStruct((4, ROW, half, WIDTH), jnp.float32)] * 2,
        compiler_params=pltpu.CompilerParams(dimension_semantics=("arbitrary",), vmem_limit_bytes=60 * MIB),
        cost_estimate=LONG,
    )(table, inputs, turned, *after)


def products(inputs, turned, table, count, strip_of, wanted, after):
    depth = inputs.shape[0]

    def body(table, x, k, *refs):
        outs = refs[len(after) :]
        step = pl.program_id(0)
        for (low, height, first, number, _), out in zip(wanted, outs):

            def emit(low=low, height=height, out=out):
                value = jnp.dot(k[low : low + height, :], x[...], preferred_element_type=jnp.float32)
                for place in range(ROW):
                    out[0, (place - table[STRIPS]) & (ROW - 1)] = value[:, place * WIDTH : (place + 1) * WIDTH]

            if number == count:
                emit()
            else:
                pl.when((step >= first) & (step < first + number))(emit)

    def out_spec(low, height, first, number, order):
        def at(i, table):
            n = jnp.clip(i - first, 0, number - 1)
            return (n if order > 0 else number - 1 - n, 0, 0, 0)

        return pl.BlockSpec((1, ROW, height, WIDTH), at)

    return pl.pallas_call(
        body,
        grid_spec=pltpu.PrefetchScalarGridSpec(
            num_scalar_prefetch=1,
            grid=(count,),
            in_specs=[
                pl.BlockSpec((depth, STRIP), lambda i, table: (0, table[strip_of(i)])),
                pl.BlockSpec(memory_space=pltpu.VMEM),
            ]
            + [pl.BlockSpec(memory_space=pl.ANY)] * len(after),
            out_specs=[out_spec(*w) for w in wanted],
        ),
        out_shape=[jax.ShapeDtypeStruct((w[3], ROW, w[1], WIDTH), jnp.float32) for w in wanted],
        compiler_params=pltpu.CompilerParams(dimension_semantics=("arbitrary",), vmem_limit_bytes=60 * MIB),
        cost_estimate=LONG,
    )(table, inputs, turned, *after)


def combine(body, pieces, shapes, after=()):
    pieces = [p if isinstance(p, tuple) else (p, p.shape, (0,) * p.ndim) for p in pieces]

    def kernel(*refs):
        body(*refs[: len(pieces)], *refs[len(pieces) + len(after) :])

    return pl.pallas_call(
        kernel,
        grid=(1,),
        in_specs=[pl.BlockSpec(block, lambda i, at=at: at) for _, block, at in pieces]
        + [pl.BlockSpec(memory_space=pl.ANY)] * len(after),
        out_specs=[pl.BlockSpec(s, lambda i, at=(0,) * len(s): at) for s in shapes],
        out_shape=[jax.ShapeDtypeStruct(s, jnp.float32) for s in shapes],
        compiler_params=pltpu.CompilerParams(vmem_limit_bytes=60 * MIB),
        cost_estimate=SHORT,
    )(*[p[0] for p in pieces], *after)


def along(axis, array, step):
    stride = 1 if axis == "x" else 4
    pairs = [(f, f + ((f // stride + step) % 4 - f // stride % 4) * stride) for f in range(32)]
    return lax.ppermute(array, "fsdp", pairs)


def along_z(array):
    return lax.ppermute(array, "fsdp", [(f, (f + 16) % 32) for f in range(32)])


def over_x(array):
    return lax.psum_scatter(array, "fsdp", scatter_dimension=0, axis_index_groups=X_RINGS, tiled=True)[0]


def reduce_ring(axis, terms, outer, rows):
    shape = (outer, rows, WIDTH)
    count = len(terms(0, 0))

    def total(refs):
        value = refs[0][...].reshape(shape)
        for ref in refs[1:]:
            value = value + ref[...].reshape(shape)
        return value

    def first(*refs):
        up, down = refs[4 * count :]
        up[0], up[1], down[0], down[1] = [total(refs[i * count : (i + 1) * count]) for i in range(4)]

    after = yield
    pieces = terms(2, 0) + terms(1, 1) + terms(2, 1) + terms(3, 0)
    up, down = combine(first, pieces, [(2,) + shape] * 2, after)
    up_in, down_in = along(axis, up, 1), along(axis, down, -1)
    after = yield [up]

    def got(array):
        return [(array, (1,) + shape, (0, 0, 0, 0))]

    def second(*refs):
        up, down = refs[-2:]
        up[...], down[...] = total(refs[: count + 1]), total(refs[count + 1 : -2])

    pieces = terms(1, 0) + got(up_in) + terms(3, 1) + got(down_in)
    up, down = combine(second, pieces, [shape] * 2, after)
    up_last, down_last = along(axis, up, 1), along(axis, down, -1)
    yield [up], lambda half: [(down_in, 1), (up_last, None)] if half == 0 else [(up_in, 1), (down_last, None)]


def settle(low, high, write, shapes, after):
    def body(*refs):
        sums = []
        for group, pieces in ((refs[: len(low)], low), (refs[len(low) : len(low) + len(high)], high)):
            shape = [n for n in pieces[-1][1]]
            value = group[0][...].reshape(shape)
            for ref in group[1:]:
                value = value + ref[...].reshape(shape)
            sums.append(value)
        write(*sums, *refs[len(low) + len(high) :])

    return combine(body, low + high, shapes, after)


def local(params, momentum, local_params, exps, inputs, cotangent):
    groups = lax.axis_size("rep")
    group = lax.axis_index("rep")
    me = lax.axis_index("fsdp")
    at = jnp.arange(STRIPS + 1)
    table = 4 * ((me // 16 + at // 4) % 2) + (me // 4 + at) % 4
    table = jnp.where(at == STRIPS, me % 4, table).astype(jnp.int32)

    picked = jnp.sum(jnp.where(jnp.arange(groups) == group, exps, 0))
    scale_up = jnp.left_shift(1, picked).astype(jnp.float32)
    delta = params - local_params[0].astype(jnp.float32)
    coded = jnp.clip(delta * scale_up, -448.0, 448.0).astype(jnp.bfloat16)
    total = lax.psum(coded.astype(jnp.float32) / scale_up, "rep")

    half = B // 2
    b_low, b_high, c_low = A, A + half, A + B
    a, turned = all_products(inputs, cotangent, table, A)
    a_x = over_x(a).reshape(2, 4, A, WIDTH)
    b_far = products(
        inputs,
        turned,
        table,
        2,
        lambda i: 2 + 4 * i,
        [(b_low, half, 0, 2, 1), (b_high, half, 0, 2, 1)],
        [a],
    )
    b_up1, b_down1 = along("y", b_far[0], 1), along("y", b_far[1], -1)
    c_far = crossing_products(inputs, turned, table, c_low, C // 2, b_far[:1])
    c_soon, c_late = along_z(c_far[0]), along_z(c_far[1])
    c_places = {(2, 0): 0, (2, 1): 1, (1, 1): 2, (3, 0): 3, (1, 0): 4, (3, 1): 5, (0, 0): 6, (0, 1): 7}
    b_near = products(
        inputs,
        turned,
        table,
        4,
        lambda i: 1 + 4 * lax.rem(i, 2) + 2 * (i // 2),
        [(low, half, first, 2, 1) for first in (0, 2) for low in (b_low, b_high)],
        c_far[:1],
    )
    b_up2, b_down2 = along("y", b_near[1], 1), along("y", b_near[2], -1)
    *b_own, c_near = products(
        inputs,
        turned,
        table,
        5,
        lambda i: jnp.where(i == 0, 4, i - 1),
        [(b_low, half, 0, 2, -1), (b_high, half, 0, 2, -1), (c_low, C, 1, 4, 1)],
        b_near[:1],
    )

    def b_third(near_up, near_down, got_up, got_down, up, down):
        up[...] = near_up[...] + got_up[...]
        down[...] = near_down[...] + got_down[...]

    b_last = combine(b_third, [b_near[0], b_near[3], b_up1, b_down1], [(2, ROW, half, WIDTH)] * 2, [c_near])
    b_up3, b_down3 = along("y", b_last[0], 1), along("y", b_last[1], -1)

    def b_terms(dx, h):
        arrays = (b_own[0], b_down2, b_up3) if h == 0 else (b_own[1], b_up2, b_down3)
        return [(array, (2, 1, half, WIDTH), (0, dx, 0, 0)) for array in arrays]

    def c_terms(dy, h):
        block = (1, ROW, C // 2, WIDTH)
        place = c_places[dy, h]
        return [(c_near, block, (dy, 0, h, 0)), ((c_soon, c_late)[place // 4], block, (place % 4, 0, 0, 0))]

    def a_terms(dy, h):
        return [(a_x, (2, 1, A // 2, WIDTH), (0, dy, h, 0))]

    def whole(arrived):
        return [
            (array, array.shape, (0,) * 3) if n is None else (array, (1,) + array.shape[1:], (n, 0, 0, 0))
            for array, n in arrived
        ]

    def nesterov(weights, moment, total, new_weights, fresh):
        outer_grad = total[...] / groups
        fresh[...] = 0.9 * moment[...] + outer_grad
        new_weights[...] = weights[...] - 0.7 * (outer_grad + 0.9 * fresh[...])

    new_params, new_momentum = combine(nesterov, [params, momentum, total], [params.shape] * 2, b_last[:1])

    ring_b = reduce_ring("x", b_terms, 2, half)
    ring_c = reduce_ring("y", c_terms, ROW, C // 2)
    ring_a = reduce_ring("y", a_terms, 2, A // 2)
    next(ring_b), next(ring_c), next(ring_a)
    done = ring_c.send([new_params])
    done = ring_b.send(done)
    done, c_got = ring_c.send(done)
    done = ring_a.send(done)
    done, b_got = ring_b.send(done)

    def c_x_terms(dx, h):
        block = (1, 1, C // 2, WIDTH)
        terms = [(c_near, block, (0, dx, h, 0)), (c_late, block, (2 + h, dx, 0, 0))]
        for array, n in c_got(h):
            terms.append((array, block[1:], (dx, 0, 0)) if n is None else (array, block, (n, dx, 0, 0)))
        return terms

    def keep_and_cross(low, high, keep, cross):
        rows = low.shape[1]
        keep[:rows, :], keep[rows:, :] = low[0], high[0]
        cross[:rows, :], cross[rows:, :] = low[1], high[1]

    ring_cx = reduce_ring("x", c_x_terms, 1, C // 2)
    next(ring_cx)
    done = ring_cx.send(done)
    b_keep, b_cross = settle(
        b_terms(0, 0) + whole(b_got(0)), b_terms(0, 1) + whole(b_got(1)), keep_and_cross, [(B, WIDTH)] * 2, done
    )
    b_in = along_z(b_cross)
    done, cx_got = ring_cx.send([b_keep])
    done, a_got = ring_a.send(done)

    def c_home(low, high, out):
        out[: C // 2, :], out[C // 2 :, :] = low[0], high[0]

    (c_own,) = settle(
        c_x_terms(0, 0) + whole(cx_got(0)), c_x_terms(0, 1) + whole(cx_got(1)), c_home, [(C, WIDTH)], done
    )
    a_keep, a_cross = settle(
        a_terms(0, 0) + whole(a_got(0)), a_terms(0, 1) + whole(a_got(1)), keep_and_cross, [(A, WIDTH)] * 2, [c_own, b_in]
    )
    a_in = along_z(a_cross)

    def assemble(keep_a, got_a, keep_b, got_b, own_c, out):
        value = jnp.concatenate([keep_a[...] + got_a[...], keep_b[...] + got_b[...], own_c[...]], axis=0)
        out[0] = value.T

    (kv_grad,) = combine(
        assemble, [a_keep, a_in, b_keep, b_in, c_own], [(1, WIDTH, A + B + C)]
    )
    return (new_params, new_momentum, kv_grad)


def solution(mesh):
    in_specs = (
        P("fsdp", None),
        P("fsdp", None),
        P("rep", "fsdp", None),
        P(),
        P(("rep", "fsdp"), None),
        P(("rep", "fsdp"), None),
    )
    out_specs = (P("fsdp", None), P("fsdp", None), P("rep", "fsdp", None))
    return jax.shard_map(local, mesh=mesh, in_specs=in_specs, out_specs=out_specs, check_vma=False)
```

```python
import jax
import jax.numpy as jnp
from jax import lax
from jax.experimental import pallas as pl
from jax.experimental.pallas import tpu as pltpu
from jax.sharding import PartitionSpec as P

WIDTH = 256
ROW = 4
STRIP = ROW * WIDTH
STRIPS = 8
A = 384
B = 320
C = 320
X_RINGS = [[16 * z + 4 * y + x for x in range(4)] for z in range(2) for y in range(4)]
LONG = pl.CostEstimate(flops=2 * 10**10, bytes_accessed=1000, transcendentals=0)
SHORT = pl.CostEstimate(flops=4 * 10**9, bytes_accessed=1000, transcendentals=0)
MIB = 1024 * 1024


def all_products(inputs, cotangent, table, height):
    depth, columns = cotangent.shape

    def body(table, x, k, out, turned):
        step = pl.program_id(0)

        @pl.when(step == 0)
        def _():
            turned[...] = k[...].T

        value = jnp.dot(turned[:height, :], x[...], preferred_element_type=jnp.float32)
        for place in range(ROW):
            out[place, 0] = value[:, place * WIDTH : (place + 1) * WIDTH]

    out, turned = pl.pallas_call(
        body,
        grid_spec=pltpu.PrefetchScalarGridSpec(
            num_scalar_prefetch=1,
            grid=(STRIPS,),
            in_specs=[
                pl.BlockSpec((depth, STRIP), lambda i, table: (0, table[i])),
                pl.BlockSpec((depth, columns), lambda i, table: (0, 0), pipeline_mode=pl.Buffered(1)),
            ],
            out_specs=[
                pl.BlockSpec((ROW, 1, height, WIDTH), lambda i, table: (0, i, 0, 0)),
                pl.BlockSpec(memory_space=pltpu.VMEM),
            ],
        ),
        out_shape=[
            jax.ShapeDtypeStruct((ROW, STRIPS, height, WIDTH), jnp.float32),
            pltpu.VMEM((columns, depth), cotangent.dtype),
        ],
        compiler_params=pltpu.CompilerParams(dimension_semantics=("arbitrary",), vmem_limit_bytes=60 * MIB),
        cost_estimate=LONG,
    )(table, inputs, cotangent)
    return out, pltpu.with_memory_space_constraint(turned, pltpu.VMEM)


def crossing_products(inputs, turned, table, low, half, after):
    depth = inputs.shape[0]

    def body(table, x, k, *refs):
        soon, later, last = refs[-3:]
        step = pl.program_id(0)

        def emit(h, out, n):
            value = jnp.dot(k[low + h * half : low + (h + 1) * half, :], x[...], preferred_element_type=jnp.float32)
            for place in range(ROW):
                out[n, (place - table[STRIPS]) & (ROW - 1)] = value[:, place * WIDTH : (place + 1) * WIDTH]

        for at, first, second in ((0, soon, soon), (1, later, soon), (2, soon, later), (3, last, last)):

            @pl.when(step == at)
            def _(at=at, first=first, second=second):
                emit(0, first, 1 if at == 2 else 0)
                emit(1, second, 0 if at == 1 else 1)

    block = (2, ROW, half, WIDTH)
    return pl.pallas_call(
        body,
        grid_spec=pltpu.PrefetchScalarGridSpec(
            num_scalar_prefetch=1,
            grid=(4,),
            in_specs=[
                pl.BlockSpec(
                    (depth, STRIP),
                    lambda i, table: (0, table[4 + jnp.where(i == 0, 2, jnp.where(i == 3, 0, 2 * i - 1))]),
                ),
                pl.BlockSpec(memory_space=pltpu.VMEM),
            ]
            + [pl.BlockSpec(memory_space=pl.ANY)] * len(after),
            out_specs=[
                pl.BlockSpec(block, lambda i, table: (jnp.minimum(i, 1), 0, 0, 0)),
                pl.BlockSpec(block, lambda i, table: (0, 0, 0, 0)),
                pl.BlockSpec(block, lambda i, table: (0, 0, 0, 0)),
            ],
        ),
        out_shape=[jax.ShapeDtypeStruct((n, ROW, half, WIDTH), jnp.float32) for n in (4, 2, 2)],
        compiler_params=pltpu.CompilerParams(dimension_semantics=("arbitrary",), vmem_limit_bytes=60 * MIB),
        cost_estimate=LONG,
    )(table, inputs, turned, *after)


def products(inputs, turned, table, count, strip_of, wanted, after):
    depth = inputs.shape[0]

    def body(table, x, k, *refs):
        outs = refs[len(after) :]
        step = pl.program_id(0)
        for (low, height, first, number, _), out in zip(wanted, outs):

            def emit(low=low, height=height, out=out):
                value = jnp.dot(k[low : low + height, :], x[...], preferred_element_type=jnp.float32)
                for place in range(ROW):
                    out[0, (place - table[STRIPS]) & (ROW - 1)] = value[:, place * WIDTH : (place + 1) * WIDTH]

            if number == count:
                emit()
            else:
                pl.when((step >= first) & (step < first + number))(emit)

    def out_spec(low, height, first, number, order):
        def at(i, table):
            n = jnp.clip(i - first, 0, number - 1)
            return (n if order > 0 else number - 1 - n, 0, 0, 0)

        return pl.BlockSpec((1, ROW, height, WIDTH), at)

    return pl.pallas_call(
        body,
        grid_spec=pltpu.PrefetchScalarGridSpec(
            num_scalar_prefetch=1,
            grid=(count,),
            in_specs=[
                pl.BlockSpec((depth, STRIP), lambda i, table: (0, table[strip_of(i)])),
                pl.BlockSpec(memory_space=pltpu.VMEM),
            ]
            + [pl.BlockSpec(memory_space=pl.ANY)] * len(after),
            out_specs=[out_spec(*w) for w in wanted],
        ),
        out_shape=[jax.ShapeDtypeStruct((w[3], ROW, w[1], WIDTH), jnp.float32) for w in wanted],
        compiler_params=pltpu.CompilerParams(dimension_semantics=("arbitrary",), vmem_limit_bytes=60 * MIB),
        cost_estimate=LONG,
    )(table, inputs, turned, *after)


def combine(body, pieces, shapes, after=()):
    pieces = [p if isinstance(p, tuple) else (p, p.shape, (0,) * p.ndim) for p in pieces]

    def kernel(*refs):
        body(*refs[: len(pieces)], *refs[len(pieces) + len(after) :])

    return pl.pallas_call(
        kernel,
        grid=(1,),
        in_specs=[pl.BlockSpec(block, lambda i, at=at: at) for _, block, at in pieces]
        + [pl.BlockSpec(memory_space=pl.ANY)] * len(after),
        out_specs=[pl.BlockSpec(s, lambda i, at=(0,) * len(s): at) for s in shapes],
        out_shape=[jax.ShapeDtypeStruct(s, jnp.float32) for s in shapes],
        compiler_params=pltpu.CompilerParams(vmem_limit_bytes=60 * MIB),
        cost_estimate=SHORT,
    )(*[p[0] for p in pieces], *after)


def along(axis, array, step):
    stride = 1 if axis == "x" else 4
    pairs = [(f, f + ((f // stride + step) % 4 - f // stride % 4) * stride) for f in range(32)]
    return lax.ppermute(array, "fsdp", pairs)


def along_z(array):
    return lax.ppermute(array, "fsdp", [(f, (f + 16) % 32) for f in range(32)])


def over_x(array):
    return lax.psum_scatter(array, "fsdp", scatter_dimension=0, axis_index_groups=X_RINGS, tiled=True)[0]


def reduce_ring(axis, terms, outer, rows):
    shape = (outer, rows, WIDTH)
    count = len(terms(0, 0))

    def total(refs):
        value = refs[0][...].reshape(shape)
        for ref in refs[1:]:
            value = value + ref[...].reshape(shape)
        return value

    def first(*refs):
        up, down = refs[4 * count :]
        up[0], up[1], down[0], down[1] = [total(refs[i * count : (i + 1) * count]) for i in range(4)]

    after = yield
    pieces = terms(2, 0) + terms(1, 1) + terms(2, 1) + terms(3, 0)
    up, down = combine(first, pieces, [(2,) + shape] * 2, after)
    up_in, down_in = along(axis, up, 1), along(axis, down, -1)
    after = yield [up]

    def got(array):
        return [(array, (1,) + shape, (0, 0, 0, 0))]

    def second(*refs):
        up, down = refs[-2:]
        up[...], down[...] = total(refs[: count + 1]), total(refs[count + 1 : -2])

    pieces = terms(1, 0) + got(up_in) + terms(3, 1) + got(down_in)
    up, down = combine(second, pieces, [shape] * 2, after)
    up_last, down_last = along(axis, up, 1), along(axis, down, -1)
    yield [up], lambda half: [(down_in, 1), (up_last, None)] if half == 0 else [(up_in, 1), (down_last, None)]


def settle(low, high, write, shapes, after):
    def body(*refs):
        sums = []
        for group, pieces in ((refs[: len(low)], low), (refs[len(low) : len(low) + len(high)], high)):
            shape = [n for n in pieces[-1][1]]
            value = group[0][...].reshape(shape)
            for ref in group[1:]:
                value = value + ref[...].reshape(shape)
            sums.append(value)
        write(*sums, *refs[len(low) + len(high) :])

    return combine(body, low + high, shapes, after)


def local(params, momentum, local_params, exps, inputs, cotangent):
    groups = lax.axis_size("rep")
    group = lax.axis_index("rep")
    me = lax.axis_index("fsdp")
    at = jnp.arange(STRIPS + 1)
    table = 4 * ((me // 16 + at // 4) % 2) + (me // 4 + at) % 4
    table = jnp.where(at == STRIPS, me % 4, table).astype(jnp.int32)

    picked = jnp.sum(jnp.where(jnp.arange(groups) == group, exps, 0))
    scale_up = jnp.left_shift(1, picked).astype(jnp.float32)
    delta = params - local_params[0].astype(jnp.float32)
    coded = jnp.clip(delta * scale_up, -448.0, 448.0).astype(jnp.bfloat16)
    total = lax.psum(coded.astype(jnp.float32) / scale_up, "rep")

    half = B // 2
    b_low, b_high, c_low = A, A + half, A + B
    a, turned = all_products(inputs, cotangent, table, A)
    a_x = over_x(a).reshape(2, 4, A, WIDTH)
    b_far = products(
        inputs,
        turned,
        table,
        2,
        lambda i: 2 + 4 * i,
        [(b_low, half, 0, 2, 1), (b_high, half, 0, 2, 1)],
        [a],
    )
    b_up1, b_down1 = along("y", b_far[0], 1), along("y", b_far[1], -1)
    c_far = crossing_products(inputs, turned, table, c_low, C // 2, b_far[:1])
    c_z = [along_z(array) for array in c_far]
    c_places = {(2, 0): (0, 0), (2, 1): (0, 1), (1, 1): (0, 2), (3, 0): (0, 3)}
    c_places |= {(1, 0): (1, 0), (3, 1): (1, 1), (0, 0): (2, 0), (0, 1): (2, 1)}
    b_near = products(
        inputs,
        turned,
        table,
        4,
        lambda i: 1 + 4 * lax.rem(i, 2) + 2 * (i // 2),
        [(low, half, first, 2, 1) for first in (0, 2) for low in (b_low, b_high)],
        c_far[:1],
    )
    b_up2, b_down2 = along("y", b_near[1], 1), along("y", b_near[2], -1)
    *b_own, c_near = products(
        inputs,
        turned,
        table,
        5,
        lambda i: jnp.where(i == 0, 4, i - 1),
        [(b_low, half, 0, 2, -1), (b_high, half, 0, 2, -1), (c_low, C, 1, 4, 1)],
        b_near[:1],
    )

    def b_third(near_up, near_down, got_up, got_down, up, down):
        up[...] = near_up[...] + got_up[...]
        down[...] = near_down[...] + got_down[...]

    b_last = combine(b_third, [b_near[0], b_near[3], b_up1, b_down1], [(2, ROW, half, WIDTH)] * 2, [c_near])
    b_up3, b_down3 = along("y", b_last[0], 1), along("y", b_last[1], -1)

    def b_terms(dx, h):
        arrays = (b_own[0], b_down2, b_up3) if h == 0 else (b_own[1], b_up2, b_down3)
        return [(array, (2, 1, half, WIDTH), (0, dx, 0, 0)) for array in arrays]

    def c_terms(dy, h):
        block = (1, ROW, C // 2, WIDTH)
        array, n = c_places[dy, h]
        return [(c_near, block, (dy, 0, h, 0)), (c_z[array], block, (n, 0, 0, 0))]

    def a_terms(dy, h):
        return [(a_x, (2, 1, A // 2, WIDTH), (0, dy, h, 0))]

    def whole(arrived):
        return [
            (array, array.shape, (0,) * 3) if n is None else (array, (1,) + array.shape[1:], (n, 0, 0, 0))
            for array, n in arrived
        ]

    def nesterov(weights, moment, total, new_weights, fresh):
        outer_grad = total[...] / groups
        fresh[...] = 0.9 * moment[...] + outer_grad
        new_weights[...] = weights[...] - 0.7 * (outer_grad + 0.9 * fresh[...])

    new_params, new_momentum = combine(nesterov, [params, momentum, total], [params.shape] * 2, b_last[:1])

    ring_b = reduce_ring("x", b_terms, 2, half)
    ring_c = reduce_ring("y", c_terms, ROW, C // 2)
    ring_a = reduce_ring("y", a_terms, 2, A // 2)
    next(ring_b), next(ring_c), next(ring_a)
    done = ring_c.send([new_params])
    done = ring_b.send(done)
    done, c_got = ring_c.send(done)
    done = ring_a.send(done)
    done, b_got = ring_b.send(done)

    def c_x_terms(dx, h):
        block = (1, 1, C // 2, WIDTH)
        terms = [(c_near, block, (0, dx, h, 0)), (c_z[2], block, (h, dx, 0, 0))]
        for array, n in c_got(h):
            terms.append((array, block[1:], (dx, 0, 0)) if n is None else (array, block, (n, dx, 0, 0)))
        return terms

    def keep_and_cross(low, high, keep, cross):
        rows = low.shape[1]
        keep[:rows, :], keep[rows:, :] = low[0], high[0]
        cross[:rows, :], cross[rows:, :] = low[1], high[1]

    ring_cx = reduce_ring("x", c_x_terms, 1, C // 2)
    next(ring_cx)
    done = ring_cx.send(done)
    b_keep, b_cross = settle(
        b_terms(0, 0) + whole(b_got(0)), b_terms(0, 1) + whole(b_got(1)), keep_and_cross, [(B, WIDTH)] * 2, done
    )
    b_in = along_z(b_cross)
    done, cx_got = ring_cx.send([b_keep])
    done, a_got = ring_a.send(done)

    def c_home(low, high, out):
        out[: C // 2, :], out[C // 2 :, :] = low[0], high[0]

    (c_own,) = settle(
        c_x_terms(0, 0) + whole(cx_got(0)), c_x_terms(0, 1) + whole(cx_got(1)), c_home, [(C, WIDTH)], done
    )
    a_keep, a_cross = settle(
        a_terms(0, 0) + whole(a_got(0)), a_terms(0, 1) + whole(a_got(1)), keep_and_cross, [(A, WIDTH)] * 2, [c_own, b_in]
    )
    a_in = along_z(a_cross)

    def assemble(keep_a, got_a, keep_b, got_b, own_c, out):
        value = jnp.concatenate([keep_a[...] + got_a[...], keep_b[...] + got_b[...], own_c[...]], axis=0)
        out[0] = value.T

    (kv_grad,) = combine(
        assemble, [a_keep, a_in, b_keep, b_in, c_own], [(1, WIDTH, A + B + C)]
    )
    return (new_params, new_momentum, kv_grad)


def solution(mesh):
    in_specs = (
        P("fsdp", None),
        P("fsdp", None),
        P("rep", "fsdp", None),
        P(),
        P(("rep", "fsdp"), None),
        P(("rep", "fsdp"), None),
    )
    out_specs = (P("fsdp", None), P("fsdp", None), P("rep", "fsdp", None))
    return jax.shard_map(local, mesh=mesh, in_specs=in_specs, out_specs=out_specs, check_vma=False)
```

```python
import jax
import jax.numpy as jnp
from jax import lax
from jax.experimental import pallas as pl
from jax.experimental.pallas import tpu as pltpu
from jax.sharding import PartitionSpec as P

WIDTH = 256
ROW = 4
STRIP = ROW * WIDTH
STRIPS = 8
A = 384
B = 320
C = 320
X_RINGS = [[16 * z + 4 * y + x for x in range(4)] for z in range(2) for y in range(4)]
LONG = pl.CostEstimate(flops=2 * 10**10, bytes_accessed=1000, transcendentals=0)
SHORT = pl.CostEstimate(flops=4 * 10**9, bytes_accessed=1000, transcendentals=0)
MIB = 1024 * 1024


def all_products(inputs, cotangent, table, height):
    depth, columns = cotangent.shape

    def body(table, x, k, out, turned):
        step = pl.program_id(0)

        @pl.when(step == 0)
        def _():
            turned[...] = k[...].T

        value = jnp.dot(turned[:height, :], x[...], preferred_element_type=jnp.float32)
        for place in range(ROW):
            out[place, 0] = value[:, place * WIDTH : (place + 1) * WIDTH]

    out, turned = pl.pallas_call(
        body,
        grid_spec=pltpu.PrefetchScalarGridSpec(
            num_scalar_prefetch=1,
            grid=(STRIPS,),
            in_specs=[
                pl.BlockSpec((depth, STRIP), lambda i, table: (0, table[i])),
                pl.BlockSpec((depth, columns), lambda i, table: (0, 0), pipeline_mode=pl.Buffered(1)),
            ],
            out_specs=[
                pl.BlockSpec((ROW, 1, height, WIDTH), lambda i, table: (0, i, 0, 0)),
                pl.BlockSpec(memory_space=pltpu.VMEM),
            ],
        ),
        out_shape=[
            jax.ShapeDtypeStruct((ROW, STRIPS, height, WIDTH), jnp.float32),
            pltpu.VMEM((columns, depth), cotangent.dtype),
        ],
        compiler_params=pltpu.CompilerParams(dimension_semantics=("arbitrary",), vmem_limit_bytes=60 * MIB),
        cost_estimate=LONG,
    )(table, inputs, cotangent)
    return out, pltpu.with_memory_space_constraint(turned, pltpu.VMEM)


def crossing_products(inputs, turned, table, low, half, after):
    depth = inputs.shape[0]

    def body(table, x, k, *refs):
        soon, later, last = refs[-3:]
        step = pl.program_id(0)

        def emit(h, out, n):
            value = jnp.dot(k[low + h * half : low + (h + 1) * half, :], x[...], preferred_element_type=jnp.float32)
            for place in range(ROW):
                out[n, place] = value[:, place * WIDTH : (place + 1) * WIDTH]

        for at, first, second in ((0, soon, soon), (1, later, soon), (2, soon, later), (3, last, last)):

            @pl.when(step == at)
            def _(at=at, first=first, second=second):
                emit(0, first, 1 if at == 2 else 0)
                emit(1, second, 0 if at == 1 else 1)

    block = (2, ROW, half, WIDTH)
    return pl.pallas_call(
        body,
        grid_spec=pltpu.PrefetchScalarGridSpec(
            num_scalar_prefetch=1,
            grid=(4,),
            in_specs=[
                pl.BlockSpec(
                    (depth, STRIP),
                    lambda i, table: (0, table[4 + jnp.where(i == 0, 2, jnp.where(i == 3, 0, 2 * i - 1))]),
                ),
                pl.BlockSpec(memory_space=pltpu.VMEM),
            ]
            + [pl.BlockSpec(memory_space=pl.ANY)] * len(after),
            out_specs=[
                pl.BlockSpec(block, lambda i, table: (jnp.minimum(i, 1), 0, 0, 0)),
                pl.BlockSpec(block, lambda i, table: (0, 0, 0, 0)),
                pl.BlockSpec(block, lambda i, table: (0, 0, 0, 0)),
            ],
        ),
        out_shape=[jax.ShapeDtypeStruct((n, ROW, half, WIDTH), jnp.float32) for n in (4, 2, 2)],
        compiler_params=pltpu.CompilerParams(dimension_semantics=("arbitrary",), vmem_limit_bytes=60 * MIB),
        cost_estimate=LONG,
    )(table, inputs, turned, *after)


def products(inputs, turned, table, count, strip_of, wanted, after):
    depth = inputs.shape[0]

    def body(table, x, k, *refs):
        outs = refs[len(after) :]
        step = pl.program_id(0)
        for (low, height, first, number, _), out in zip(wanted, outs):

            def emit(low=low, height=height, out=out):
                value = jnp.dot(k[low : low + height, :], x[...], preferred_element_type=jnp.float32)
                for place in range(ROW):
                    out[0, place] = value[:, place * WIDTH : (place + 1) * WIDTH]

            if number == count:
                emit()
            else:
                pl.when((step >= first) & (step < first + number))(emit)

    def out_spec(low, height, first, number, order):
        def at(i, table):
            n = jnp.clip(i - first, 0, number - 1)
            return (n if order > 0 else number - 1 - n, 0, 0, 0)

        return pl.BlockSpec((1, ROW, height, WIDTH), at)

    return pl.pallas_call(
        body,
        grid_spec=pltpu.PrefetchScalarGridSpec(
            num_scalar_prefetch=1,
            grid=(count,),
            in_specs=[
                pl.BlockSpec((depth, STRIP), lambda i, table: (0, table[strip_of(i)])),
                pl.BlockSpec(memory_space=pltpu.VMEM),
            ]
            + [pl.BlockSpec(memory_space=pl.ANY)] * len(after),
            out_specs=[out_spec(*w) for w in wanted],
        ),
        out_shape=[jax.ShapeDtypeStruct((w[3], ROW, w[1], WIDTH), jnp.float32) for w in wanted],
        compiler_params=pltpu.CompilerParams(dimension_semantics=("arbitrary",), vmem_limit_bytes=60 * MIB),
        cost_estimate=LONG,
    )(table, inputs, turned, *after)


def combine(body, pieces, shapes, after=()):
    pieces = [p if isinstance(p, tuple) else (p, p.shape, (0,) * p.ndim) for p in pieces]

    def kernel(*refs):
        body(*refs[: len(pieces)], *refs[len(pieces) + len(after) :])

    return pl.pallas_call(
        kernel,
        grid=(1,),
        in_specs=[pl.BlockSpec(block, lambda i, at=at: at) for _, block, at in pieces]
        + [pl.BlockSpec(memory_space=pl.ANY)] * len(after),
        out_specs=[pl.BlockSpec(s, lambda i, at=(0,) * len(s): at) for s in shapes],
        out_shape=[jax.ShapeDtypeStruct(s, jnp.float32) for s in shapes],
        compiler_params=pltpu.CompilerParams(vmem_limit_bytes=60 * MIB),
        cost_estimate=SHORT,
    )(*[p[0] for p in pieces], *after)


def along_y(array, step):
    pairs = [(f, f + ((f // 4 + step) % 4 - f // 4 % 4) * 4) for f in range(32)]
    return lax.ppermute(array, "fsdp", pairs)


def along_z(array):
    return lax.ppermute(array, "fsdp", [(f, (f + 16) % 32) for f in range(32)])


def over_x(array):
    return lax.psum_scatter(array, "fsdp", scatter_dimension=0, axis_index_groups=X_RINGS, tiled=True)[0]


def reduce_ring(terms, outer, rows):
    shape = (outer, rows, WIDTH)
    count = len(terms(0, 0))

    def total(refs):
        value = refs[0][...].reshape(shape)
        for ref in refs[1:]:
            value = value + ref[...].reshape(shape)
        return value

    def first(*refs):
        up, down = refs[4 * count :]
        up[0], up[1], down[0], down[1] = [total(refs[i * count : (i + 1) * count]) for i in range(4)]

    after = yield
    pieces = terms(2, 0) + terms(1, 1) + terms(2, 1) + terms(3, 0)
    up, down = combine(first, pieces, [(2,) + shape] * 2, after)
    up_in, down_in = along_y(up, 1), along_y(down, -1)
    after = yield [up]

    def got(array):
        return [(array, (1,) + shape, (0, 0, 0, 0))]

    def second(*refs):
        up, down = refs[-2:]
        up[...], down[...] = total(refs[: count + 1]), total(refs[count + 1 : -2])

    pieces = terms(1, 0) + got(up_in) + terms(3, 1) + got(down_in)
    up, down = combine(second, pieces, [shape] * 2, after)
    up_last, down_last = along_y(up, 1), along_y(down, -1)
    yield [up], lambda half: [(down_in, 1), (up_last, None)] if half == 0 else [(up_in, 1), (down_last, None)]


def settle(low, high, write, shapes, after):
    def body(*refs):
        sums = []
        for group, pieces in ((refs[: len(low)], low), (refs[len(low) : len(low) + len(high)], high)):
            shape = [n for n in pieces[-1][1]]
            value = group[0][...].reshape(shape)
            for ref in group[1:]:
                value = value + ref[...].reshape(shape)
            sums.append(value)
        write(*sums, *refs[len(low) + len(high) :])

    return combine(body, low + high, shapes, after)


def local(params, momentum, local_params, exps, inputs, cotangent):
    groups = lax.axis_size("rep")
    group = lax.axis_index("rep")
    me = lax.axis_index("fsdp")
    at = jnp.arange(STRIPS)
    table = (4 * ((me // 16 + at // 4) % 2) + (me // 4 + at) % 4).astype(jnp.int32)

    picked = jnp.sum(jnp.where(jnp.arange(groups) == group, exps, 0))
    scale_up = jnp.left_shift(1, picked).astype(jnp.float32)
    delta = params - local_params[0].astype(jnp.float32)
    coded = jnp.clip(delta * scale_up, -448.0, 448.0).astype(jnp.bfloat16)
    total = lax.psum(coded.astype(jnp.float32) / scale_up, "rep")

    half = B // 2
    b_low, b_high, c_low = A, A + half, A + B
    a, turned = all_products(inputs, cotangent, table, A)
    a_x = over_x(a).reshape(2, 4, A, WIDTH)
    b_far = products(
        inputs,
        turned,
        table,
        2,
        lambda i: 2 + 4 * i,
        [(b_low, half, 0, 2, 1), (b_high, half, 0, 2, 1)],
        [a],
    )
    b_up1, b_down1 = along_y(b_far[0], 1), along_y(b_far[1], -1)
    c_far = crossing_products(inputs, turned, table, c_low, C // 2, b_far[:1])
    c_z = [along_z(array) for array in c_far]
    c_places = {(2, 0): (0, 0), (2, 1): (0, 1), (1, 1): (0, 2), (3, 0): (0, 3)}
    c_places |= {(1, 0): (1, 0), (3, 1): (1, 1), (0, 0): (2, 0), (0, 1): (2, 1)}
    b_near = products(
        inputs,
        turned,
        table,
        4,
        lambda i: 1 + 4 * lax.rem(i, 2) + 2 * (i // 2),
        [(low, half, first, 2, 1) for first in (0, 2) for low in (b_low, b_high)],
        c_far[:1],
    )
    b_up2, b_down2 = along_y(b_near[1], 1), along_y(b_near[2], -1)
    *b_own, c_near = products(
        inputs,
        turned,
        table,
        5,
        lambda i: jnp.where(i == 0, 4, i - 1),
        [(b_low, half, 0, 2, -1), (b_high, half, 0, 2, -1), (c_low, C, 1, 4, 1)],
        b_near[:1],
    )

    def b_third(near_up, near_down, got_up, got_down, up, down):
        up[...] = near_up[...] + got_up[...]
        down[...] = near_down[...] + got_down[...]

    b_last = combine(b_third, [b_near[0], b_near[3], b_up1, b_down1], [(2, ROW, half, WIDTH)] * 2, [c_near])
    b_up3, b_down3 = along_y(b_last[0], 1), along_y(b_last[1], -1)

    def b_home(own0, own1, up2, down2, up3, down3, out):
        for z in range(2):
            for x in range(ROW):
                low = B * z
                out[x, low : low + half, :] = own0[z, x] + down2[z, x] + up3[z, x]
                out[x, low + half : low + B, :] = own1[z, x] + up2[z, x] + down3[z, x]

    def c_terms(dy, h):
        block = (1, ROW, C // 2, WIDTH)
        array, n = c_places[dy, h]
        return [(c_near, block, (dy, 0, h, 0)), (c_z[array], block, (n, 0, 0, 0))]

    def a_terms(dy, h):
        return [(a_x, (2, 1, A // 2, WIDTH), (0, dy, h, 0))]

    def whole(arrived):
        return [
            (array, array.shape, (0,) * 3) if n is None else (array, (1,) + array.shape[1:], (n, 0, 0, 0))
            for array, n in arrived
        ]

    def nesterov(weights, moment, total, new_weights, fresh):
        outer_grad = total[...] / groups
        fresh[...] = 0.9 * moment[...] + outer_grad
        new_weights[...] = weights[...] - 0.7 * (outer_grad + 0.9 * fresh[...])

    new_params, new_momentum = combine(nesterov, [params, momentum, total], [params.shape] * 2, b_last[:1])

    ring_c = reduce_ring(c_terms, ROW, C // 2)
    ring_a = reduce_ring(a_terms, 2, A // 2)
    next(ring_c), next(ring_a)
    done = ring_c.send([new_params])
    (b_sum,) = combine(b_home, [*b_own, b_up2, b_down2, b_up3, b_down3], [(ROW, 2 * B, WIDTH)], done)
    b_x = over_x(b_sum)
    b_in = along_z(b_x[B:])
    done = ring_a.send([b_sum])
    done, c_got = ring_c.send(done)
    done, a_got = ring_a.send(done)

    def keep_and_cross(low, high, keep, cross):
        rows = low.shape[1]
        keep[:rows, :], keep[rows:, :] = low[0], high[0]
        cross[:rows, :], cross[rows:, :] = low[1], high[1]

    def c_home(low, high, out):
        out[:, : C // 2, :], out[:, C // 2 :, :] = low, high

    (c_sum,) = settle(
        c_terms(0, 0) + whole(c_got(0)), c_terms(0, 1) + whole(c_got(1)), c_home, [(ROW, C, WIDTH)], done
    )
    c_own = over_x(c_sum)
    a_keep, a_cross = settle(
        a_terms(0, 0) + whole(a_got(0)), a_terms(0, 1) + whole(a_got(1)), keep_and_cross, [(A, WIDTH)] * 2, [c_sum, b_in]
    )
    a_in = along_z(a_cross)

    def assemble(keep_a, got_a, keep_b, got_b, own_c, out):
        value = jnp.concatenate([keep_a[...] + got_a[...], keep_b[...] + got_b[...], own_c[...]], axis=0)
        out[0] = value.T

    (kv_grad,) = combine(
        assemble, [a_keep, a_in, (b_x, (B, WIDTH), (0, 0)), b_in, c_own], [(1, WIDTH, A + B + C)]
    )
    return (new_params, new_momentum, kv_grad)


def solution(mesh):
    in_specs = (
        P("fsdp", None),
        P("fsdp", None),
        P("rep", "fsdp", None),
        P(),
        P(("rep", "fsdp"), None),
        P(("rep", "fsdp"), None),
    )
    out_specs = (P("fsdp", None), P("fsdp", None), P("rep", "fsdp", None))
    return jax.shard_map(local, mesh=mesh, in_specs=in_specs, out_specs=out_specs, check_vma=False)
```

```python
import jax
import jax.numpy as jnp
from jax import lax
from jax.experimental import pallas as pl
from jax.experimental.pallas import tpu as pltpu
from jax.sharding import PartitionSpec as P

WIDTH = 256
ROW = 4
STRIP = ROW * WIDTH
STRIPS = 8
A = 384
B = 320
C = 320
X_RINGS = [[16 * z + 4 * y + x for x in range(4)] for z in range(2) for y in range(4)]
LONG = pl.CostEstimate(flops=2 * 10**10, bytes_accessed=1000, transcendentals=0)
SHORT = pl.CostEstimate(flops=6 * 10**9, bytes_accessed=1000, transcendentals=0)
MIB = 1024 * 1024


def all_products(inputs, cotangent, table, height):
    depth, columns = cotangent.shape

    def body(table, x, k, out, turned):
        step = pl.program_id(0)

        @pl.when(step == 0)
        def _():
            turned[...] = k[...].T

        value = jnp.dot(turned[:height, :], x[...], preferred_element_type=jnp.float32)
        for place in range(ROW):
            out[place, 0] = value[:, place * WIDTH : (place + 1) * WIDTH]

    out, turned = pl.pallas_call(
        body,
        grid_spec=pltpu.PrefetchScalarGridSpec(
            num_scalar_prefetch=1,
            grid=(STRIPS,),
            in_specs=[
                pl.BlockSpec((depth, STRIP), lambda i, table: (0, table[i])),
                pl.BlockSpec((depth, columns), lambda i, table: (0, 0), pipeline_mode=pl.Buffered(1)),
            ],
            out_specs=[
                pl.BlockSpec((ROW, 1, height, WIDTH), lambda i, table: (0, i, 0, 0)),
                pl.BlockSpec(memory_space=pltpu.VMEM),
            ],
        ),
        out_shape=[
            jax.ShapeDtypeStruct((ROW, STRIPS, height, WIDTH), jnp.float32),
            pltpu.VMEM((columns, depth), cotangent.dtype),
        ],
        compiler_params=pltpu.CompilerParams(dimension_semantics=("arbitrary",), vmem_limit_bytes=60 * MIB),
        cost_estimate=LONG,
    )(table, inputs, cotangent)
    return out, pltpu.with_memory_space_constraint(turned, pltpu.VMEM)


def crossing_products(inputs, turned, table, low, half, after):
    depth = inputs.shape[0]

    def body(table, x, k, *refs):
        soon, later, last = refs[-3:]
        step = pl.program_id(0)

        def emit(h, out, n):
            value = jnp.dot(k[low + h * half : low + (h + 1) * half, :], x[...], preferred_element_type=jnp.float32)
            for place in range(ROW):
                out[n, place] = value[:, place * WIDTH : (place + 1) * WIDTH]

        for at, first, second in ((0, soon, soon), (1, later, soon), (2, soon, later), (3, last, last)):

            @pl.when(step == at)
            def _(at=at, first=first, second=second):
                emit(0, first, 1 if at == 2 else 0)
                emit(1, second, 0 if at == 1 else 1)

    block = (2, ROW, half, WIDTH)
    return pl.pallas_call(
        body,
        grid_spec=pltpu.PrefetchScalarGridSpec(
            num_scalar_prefetch=1,
            grid=(4,),
            in_specs=[
                pl.BlockSpec(
                    (depth, STRIP),
                    lambda i, table: (0, table[4 + jnp.where(i == 0, 2, jnp.where(i == 3, 0, 2 * i - 1))]),
                ),
                pl.BlockSpec(memory_space=pltpu.VMEM),
            ]
            + [pl.BlockSpec(memory_space=pl.ANY)] * len(after),
            out_specs=[
                pl.BlockSpec(block, lambda i, table: (jnp.minimum(i, 1), 0, 0, 0)),
                pl.BlockSpec(block, lambda i, table: (0, 0, 0, 0)),
                pl.BlockSpec(block, lambda i, table: (0, 0, 0, 0)),
            ],
        ),
        out_shape=[jax.ShapeDtypeStruct((n, ROW, half, WIDTH), jnp.float32) for n in (4, 2, 2)],
        compiler_params=pltpu.CompilerParams(dimension_semantics=("arbitrary",), vmem_limit_bytes=60 * MIB),
        cost_estimate=LONG,
    )(table, inputs, turned, *after)


def products(inputs, turned, table, count, strip_of, wanted, after):
    depth = inputs.shape[0]

    def body(table, x, k, *refs):
        outs = refs[len(after) :]
        step = pl.program_id(0)
        for (low, height, first, number, _), out in zip(wanted, outs):

            def emit(low=low, height=height, out=out):
                value = jnp.dot(k[low : low + height, :], x[...], preferred_element_type=jnp.float32)
                for place in range(ROW):
                    out[0, place] = value[:, place * WIDTH : (place + 1) * WIDTH]

            if number == count:
                emit()
            else:
                pl.when((step >= first) & (step < first + number))(emit)

    def out_spec(low, height, first, number, order):
        def at(i, table):
            n = jnp.clip(i - first, 0, number - 1)
            return (n if order > 0 else number - 1 - n, 0, 0, 0)

        return pl.BlockSpec((1, ROW, height, WIDTH), at)

    return pl.pallas_call(
        body,
        grid_spec=pltpu.PrefetchScalarGridSpec(
            num_scalar_prefetch=1,
            grid=(count,),
            in_specs=[
                pl.BlockSpec((depth, STRIP), lambda i, table: (0, table[strip_of(i)])),
                pl.BlockSpec(memory_space=pltpu.VMEM),
            ]
            + [pl.BlockSpec(memory_space=pl.ANY)] * len(after),
            out_specs=[out_spec(*w) for w in wanted],
        ),
        out_shape=[jax.ShapeDtypeStruct((w[3], ROW, w[1], WIDTH), jnp.float32) for w in wanted],
        compiler_params=pltpu.CompilerParams(dimension_semantics=("arbitrary",), vmem_limit_bytes=60 * MIB),
        cost_estimate=LONG,
    )(table, inputs, turned, *after)


def combine(body, pieces, shapes, after=()):
    pieces = [p if isinstance(p, tuple) else (p, p.shape, (0,) * p.ndim) for p in pieces]

    def kernel(*refs):
        body(*refs[: len(pieces)], *refs[len(pieces) + len(after) :])

    return pl.pallas_call(
        kernel,
        grid=(1,),
        in_specs=[pl.BlockSpec(block, lambda i, at=at: at) for _, block, at in pieces]
        + [pl.BlockSpec(memory_space=pl.ANY)] * len(after),
        out_specs=[pl.BlockSpec(s, lambda i, at=(0,) * len(s): at) for s in shapes],
        out_shape=[jax.ShapeDtypeStruct(s, jnp.float32) for s in shapes],
        compiler_params=pltpu.CompilerParams(vmem_limit_bytes=60 * MIB),
        cost_estimate=SHORT,
    )(*[p[0] for p in pieces], *after)


def along_y(array, step):
    pairs = [(f, f + ((f // 4 + step) % 4 - f // 4 % 4) * 4) for f in range(32)]
    return lax.ppermute(array, "fsdp", pairs)


def along_z(array):
    return lax.ppermute(array, "fsdp", [(f, (f + 16) % 32) for f in range(32)])


def over_x(array):
    return lax.psum_scatter(array, "fsdp", scatter_dimension=0, axis_index_groups=X_RINGS, tiled=True)[0]


def reduce_ring(terms, outer, rows):
    shape = (outer, rows, WIDTH)
    count = len(terms(0, 0))

    def total(refs):
        value = refs[0][...].reshape(shape)
        for ref in refs[1:]:
            value = value + ref[...].reshape(shape)
        return value

    def first(*refs):
        up, down = refs[4 * count :]
        up[0], up[1], down[0], down[1] = [total(refs[i * count : (i + 1) * count]) for i in range(4)]

    after = yield
    pieces = terms(2, 0) + terms(1, 1) + terms(2, 1) + terms(3, 0)
    up, down = combine(first, pieces, [(2,) + shape] * 2, after)
    up_in, down_in = along_y(up, 1), along_y(down, -1)
    after = yield [up]

    def got(array):
        return [(array, (1,) + shape, (0, 0, 0, 0))]

    def second(*refs):
        up, down = refs[-2:]
        up[...], down[...] = total(refs[: count + 1]), total(refs[count + 1 : -2])

    pieces = terms(1, 0) + got(up_in) + terms(3, 1) + got(down_in)
    up, down = combine(second, pieces, [shape] * 2, after)
    up_last, down_last = along_y(up, 1), along_y(down, -1)
    yield [up], lambda half: [(down_in, 1), (up_last, None)] if half == 0 else [(up_in, 1), (down_last, None)]


def settle(low, high, write, shapes, after):
    def body(*refs):
        sums = []
        for group, pieces in ((refs[: len(low)], low), (refs[len(low) : len(low) + len(high)], high)):
            shape = [n for n in pieces[-1][1]]
            value = group[0][...].reshape(shape)
            for ref in group[1:]:
                value = value + ref[...].reshape(shape)
            sums.append(value)
        write(*sums, *refs[len(low) + len(high) :])

    return combine(body, low + high, shapes, after)


def local(params, momentum, local_params, exps, inputs, cotangent):
    groups = lax.axis_size("rep")
    group = lax.axis_index("rep")
    me = lax.axis_index("fsdp")
    at = jnp.arange(STRIPS)
    table = (4 * ((me // 16 + at // 4) % 2) + (me // 4 + at) % 4).astype(jnp.int32)

    picked = jnp.sum(jnp.where(jnp.arange(groups) == group, exps, 0))
    scale_up = jnp.left_shift(1, picked).astype(jnp.float32)
    delta = params - local_params[0].astype(jnp.float32)
    coded = jnp.clip(delta * scale_up, -448.0, 448.0).astype(jnp.bfloat16)
    total = lax.psum(coded.astype(jnp.float32) / scale_up, "rep")

    half = B // 2
    b_low, b_high, c_low = A, A + half, A + B
    a, turned = all_products(inputs, cotangent, table, A)
    a_x = over_x(a).reshape(2, 4, A, WIDTH)
    b_far = products(
        inputs,
        turned,
        table,
        2,
        lambda i: 2 + 4 * i,
        [(b_low, half, 0, 2, 1), (b_high, half, 0, 2, 1)],
        [a],
    )
    b_up1, b_down1 = along_y(b_far[0], 1), along_y(b_far[1], -1)
    c_far = crossing_products(inputs, turned, table, c_low, C // 2, b_far[:1])
    c_z = [along_z(array) for array in c_far]
    c_places = {(2, 0): (0, 0), (2, 1): (0, 1), (1, 1): (0, 2), (3, 0): (0, 3)}
    c_places |= {(1, 0): (1, 0), (3, 1): (1, 1), (0, 0): (2, 0), (0, 1): (2, 1)}
    b_near = products(
        inputs,
        turned,
        table,
        4,
        lambda i: 1 + 4 * lax.rem(i, 2) + 2 * (i // 2),
        [(low, half, first, 2, 1) for first in (0, 2) for low in (b_low, b_high)],
        c_far[:1],
    )
    b_up2, b_down2 = along_y(b_near[1], 1), along_y(b_near[2], -1)
    *b_own, c_near = products(
        inputs,
        turned,
        table,
        5,
        lambda i: jnp.where(i == 0, 4, i - 1),
        [(b_low, half, 0, 2, -1), (b_high, half, 0, 2, -1), (c_low, C, 1, 4, 1)],
        b_near[:1],
    )

    def b_third(near_up, near_down, got_up, got_down, up, down):
        up[...] = near_up[...] + got_up[...]
        down[...] = near_down[...] + got_down[...]

    b_last = combine(b_third, [b_near[0], b_near[3], b_up1, b_down1], [(2, ROW, half, WIDTH)] * 2, [c_near])
    b_up3, b_down3 = along_y(b_last[0], 1), along_y(b_last[1], -1)

    def b_home(own0, own1, up2, down2, up3, down3, out):
        for z in range(2):
            for x in range(ROW):
                low = B * z
                out[x, low : low + half, :] = own0[z, x] + down2[z, x] + up3[z, x]
                out[x, low + half : low + B, :] = own1[z, x] + up2[z, x] + down3[z, x]

    def c_terms(dy, h):
        block = (1, ROW, C // 2, WIDTH)
        array, n = c_places[dy, h]
        return [(c_near, block, (dy, 0, h, 0)), (c_z[array], block, (n, 0, 0, 0))]

    def a_terms(dy, h):
        return [(a_x, (2, 1, A // 2, WIDTH), (0, dy, h, 0))]

    def whole(arrived):
        return [
            (array, array.shape, (0,) * 3) if n is None else (array, (1,) + array.shape[1:], (n, 0, 0, 0))
            for array, n in arrived
        ]

    def nesterov(weights, moment, total, new_weights, fresh):
        outer_grad = total[...] / groups
        fresh[...] = 0.9 * moment[...] + outer_grad
        new_weights[...] = weights[...] - 0.7 * (outer_grad + 0.9 * fresh[...])

    new_params, new_momentum = combine(nesterov, [params, momentum, total], [params.shape] * 2, b_last[:1])

    ring_c = reduce_ring(c_terms, ROW, C // 2)
    ring_a = reduce_ring(a_terms, 2, A // 2)
    next(ring_c), next(ring_a)
    done = ring_c.send([new_params])
    (b_sum,) = combine(b_home, [*b_own, b_up2, b_down2, b_up3, b_down3], [(ROW, 2 * B, WIDTH)], done)
    b_x = over_x(b_sum)
    b_in = along_z(b_x[B:])
    done = ring_a.send([b_sum])
    done, c_got = ring_c.send(done)
    done, a_got = ring_a.send(done)

    def keep_and_cross(low, high, keep, cross):
        rows = low.shape[1]
        keep[:rows, :], keep[rows:, :] = low[0], high[0]
        cross[:rows, :], cross[rows:, :] = low[1], high[1]

    def c_home(low, high, out):
        out[:, : C // 2, :], out[:, C // 2 :, :] = low, high

    (c_sum,) = settle(
        c_terms(0, 0) + whole(c_got(0)), c_terms(0, 1) + whole(c_got(1)), c_home, [(ROW, C, WIDTH)], done
    )
    c_own = over_x(c_sum)
    a_keep, a_cross = settle(
        a_terms(0, 0) + whole(a_got(0)), a_terms(0, 1) + whole(a_got(1)), keep_and_cross, [(A, WIDTH)] * 2, [c_sum, b_in]
    )
    a_in = along_z(a_cross)

    def assemble(keep_a, got_a, keep_b, got_b, own_c, out):
        value = jnp.concatenate([keep_a[...] + got_a[...], keep_b[...] + got_b[...], own_c[...]], axis=0)
        out[0] = value.T

    (kv_grad,) = combine(
        assemble, [a_keep, a_in, (b_x, (B, WIDTH), (0, 0)), b_in, c_own], [(1, WIDTH, A + B + C)]
    )
    return (new_params, new_momentum, kv_grad)


def solution(mesh):
    in_specs = (
        P("fsdp", None),
        P("fsdp", None),
        P("rep", "fsdp", None),
        P(),
        P(("rep", "fsdp"), None),
        P(("rep", "fsdp"), None),
    )
    out_specs = (P("fsdp", None), P("fsdp", None), P("rep", "fsdp", None))
    return jax.shard_map(local, mesh=mesh, in_specs=in_specs, out_specs=out_specs, check_vma=False)
```

```python
import jax
import jax.numpy as jnp
from jax import lax
from jax.experimental import pallas as pl
from jax.experimental.pallas import tpu as pltpu
from jax.sharding import PartitionSpec as P

WIDTH = 256
ROW = 4
STRIP = ROW * WIDTH
STRIPS = 8
A = 384
B = 320
C = 320
X_RINGS = [[16 * z + 4 * y + x for x in range(4)] for z in range(2) for y in range(4)]
LONG = pl.CostEstimate(flops=2 * 10**10, bytes_accessed=1000, transcendentals=0)
SHORT = pl.CostEstimate(flops=4 * 10**9, bytes_accessed=1000, transcendentals=0)
MIB = 1024 * 1024


def all_products(inputs, cotangent, table, height):
    depth, columns = cotangent.shape

    def body(table, x, k, out, turned):
        step = pl.program_id(0)

        @pl.when(step == 0)
        def _():
            turned[...] = k[...].T

        value = jnp.dot(turned[:height, :], x[...], preferred_element_type=jnp.float32)
        for place in range(ROW):
            out[place, 0] = value[:, place * WIDTH : (place + 1) * WIDTH]

    out, turned = pl.pallas_call(
        body,
        grid_spec=pltpu.PrefetchScalarGridSpec(
            num_scalar_prefetch=1,
            grid=(STRIPS,),
            in_specs=[
                pl.BlockSpec((depth, STRIP), lambda i, table: (0, table[i])),
                pl.BlockSpec((depth, columns), lambda i, table: (0, 0), pipeline_mode=pl.Buffered(1)),
            ],
            out_specs=[
                pl.BlockSpec((ROW, 1, height, WIDTH), lambda i, table: (0, i, 0, 0)),
                pl.BlockSpec(memory_space=pltpu.VMEM),
            ],
        ),
        out_shape=[
            jax.ShapeDtypeStruct((ROW, STRIPS, height, WIDTH), jnp.float32),
            pltpu.VMEM((columns, depth), cotangent.dtype),
        ],
        compiler_params=pltpu.CompilerParams(dimension_semantics=("arbitrary",), vmem_limit_bytes=60 * MIB),
        cost_estimate=LONG,
    )(table, inputs, cotangent)
    return out, pltpu.with_memory_space_constraint(turned, pltpu.VMEM)


def crossing_products(inputs, turned, table, low, half, after):
    depth = inputs.shape[0]

    def body(table, x, k, *refs):
        soon, later, last = refs[-3:]
        step = pl.program_id(0)

        def emit(h, out, n):
            value = jnp.dot(k[low + h * half : low + (h + 1) * half, :], x[...], preferred_element_type=jnp.float32)
            for place in range(ROW):
                out[n, place] = value[:, place * WIDTH : (place + 1) * WIDTH]

        for at, first, second in ((0, soon, soon), (1, later, soon), (2, soon, later), (3, last, last)):

            @pl.when(step == at)
            def _(at=at, first=first, second=second):
                emit(0, first, 1 if at == 2 else 0)
                emit(1, second, 0 if at == 1 else 1)

    block = (2, ROW, half, WIDTH)
    return pl.pallas_call(
        body,
        grid_spec=pltpu.PrefetchScalarGridSpec(
            num_scalar_prefetch=1,
            grid=(4,),
            in_specs=[
                pl.BlockSpec(
                    (depth, STRIP),
                    lambda i, table: (0, table[4 + jnp.where(i == 0, 2, jnp.where(i == 3, 0, 2 * i - 1))]),
                ),
                pl.BlockSpec(memory_space=pltpu.VMEM),
            ]
            + [pl.BlockSpec(memory_space=pl.ANY)] * len(after),
            out_specs=[
                pl.BlockSpec(block, lambda i, table: (jnp.minimum(i, 1), 0, 0, 0)),
                pl.BlockSpec(block, lambda i, table: (0, 0, 0, 0)),
                pl.BlockSpec(block, lambda i, table: (0, 0, 0, 0)),
            ],
        ),
        out_shape=[jax.ShapeDtypeStruct((n, ROW, half, WIDTH), jnp.float32) for n in (4, 2, 2)],
        compiler_params=pltpu.CompilerParams(dimension_semantics=("arbitrary",), vmem_limit_bytes=60 * MIB),
        cost_estimate=LONG,
    )(table, inputs, turned, *after)


def products(inputs, turned, table, count, strip_of, wanted, after):
    depth = inputs.shape[0]

    def body(table, x, k, *refs):
        outs = refs[len(after) :]
        step = pl.program_id(0)
        for (low, height, first, number, _, turn), out in zip(wanted, outs):

            def emit(low=low, height=height, turn=turn, out=out):
                value = jnp.dot(k[low : low + height, :], x[...], preferred_element_type=jnp.float32)
                for place in range(ROW):
                    out[0, (place - turn * table[STRIPS]) & (ROW - 1)] = value[:, place * WIDTH : (place + 1) * WIDTH]

            if number == count:
                emit()
            else:
                pl.when((step >= first) & (step < first + number))(emit)

    def out_spec(low, height, first, number, order, turn):
        def at(i, table):
            n = jnp.clip(i - first, 0, number - 1)
            return (n if order > 0 else number - 1 - n, 0, 0, 0)

        return pl.BlockSpec((1, ROW, height, WIDTH), at)

    return pl.pallas_call(
        body,
        grid_spec=pltpu.PrefetchScalarGridSpec(
            num_scalar_prefetch=1,
            grid=(count,),
            in_specs=[
                pl.BlockSpec((depth, STRIP), lambda i, table: (0, table[strip_of(i)])),
                pl.BlockSpec(memory_space=pltpu.VMEM),
            ]
            + [pl.BlockSpec(memory_space=pl.ANY)] * len(after),
            out_specs=[out_spec(*w) for w in wanted],
        ),
        out_shape=[jax.ShapeDtypeStruct((w[3], ROW, w[1], WIDTH), jnp.float32) for w in wanted],
        compiler_params=pltpu.CompilerParams(dimension_semantics=("arbitrary",), vmem_limit_bytes=60 * MIB),
        cost_estimate=LONG,
    )(table, inputs, turned, *after)


def combine(body, pieces, shapes, after=()):
    pieces = [p if isinstance(p, tuple) else (p, p.shape, (0,) * p.ndim) for p in pieces]

    def kernel(*refs):
        body(*refs[: len(pieces)], *refs[len(pieces) + len(after) :])

    return pl.pallas_call(
        kernel,
        grid=(1,),
        in_specs=[pl.BlockSpec(block, lambda i, at=at: at) for _, block, at in pieces]
        + [pl.BlockSpec(memory_space=pl.ANY)] * len(after),
        out_specs=[pl.BlockSpec(s, lambda i, at=(0,) * len(s): at) for s in shapes],
        out_shape=[jax.ShapeDtypeStruct(s, jnp.float32) for s in shapes],
        compiler_params=pltpu.CompilerParams(vmem_limit_bytes=60 * MIB),
        cost_estimate=SHORT,
    )(*[p[0] for p in pieces], *after)


def along(axis, array, step):
    stride = 1 if axis == "x" else 4
    pairs = [(f, f + ((f // stride + step) % 4 - f // stride % 4) * stride) for f in range(32)]
    return lax.ppermute(array, "fsdp", pairs)


def along_z(array):
    return lax.ppermute(array, "fsdp", [(f, (f + 16) % 32) for f in range(32)])


def over_x(array):
    return lax.psum_scatter(array, "fsdp", scatter_dimension=0, axis_index_groups=X_RINGS, tiled=True)[0]


def reduce_ring(axis, terms, outer, rows):
    shape = (outer, rows, WIDTH)
    count = len(terms(0, 0))

    def total(refs):
        value = refs[0][...].reshape(shape)
        for ref in refs[1:]:
            value = value + ref[...].reshape(shape)
        return value

    def first(*refs):
        up, down = refs[4 * count :]
        up[0], up[1], down[0], down[1] = [total(refs[i * count : (i + 1) * count]) for i in range(4)]

    after = yield
    pieces = terms(2, 0) + terms(1, 1) + terms(2, 1) + terms(3, 0)
    up, down = combine(first, pieces, [(2,) + shape] * 2, after)
    up_in, down_in = along(axis, up, 1), along(axis, down, -1)
    after = yield [up]

    def got(array):
        return [(array, (1,) + shape, (0, 0, 0, 0))]

    def second(*refs):
        up, down = refs[-2:]
        up[...], down[...] = total(refs[: count + 1]), total(refs[count + 1 : -2])

    pieces = terms(1, 0) + got(up_in) + terms(3, 1) + got(down_in)
    up, down = combine(second, pieces, [shape] * 2, after)
    up_last, down_last = along(axis, up, 1), along(axis, down, -1)
    yield [up], lambda half: [(down_in, 1), (up_last, None)] if half == 0 else [(up_in, 1), (down_last, None)]


def settle(low, high, write, shapes, after):
    def body(*refs):
        sums = []
        for group, pieces in ((refs[: len(low)], low), (refs[len(low) : len(low) + len(high)], high)):
            shape = [n for n in pieces[-1][1]]
            value = group[0][...].reshape(shape)
            for ref in group[1:]:
                value = value + ref[...].reshape(shape)
            sums.append(value)
        write(*sums, *refs[len(low) + len(high) :])

    return combine(body, low + high, shapes, after)


def local(params, momentum, local_params, exps, inputs, cotangent):
    groups = lax.axis_size("rep")
    group = lax.axis_index("rep")
    me = lax.axis_index("fsdp")
    at = jnp.arange(STRIPS + 1)
    table = 4 * ((me // 16 + at // 4) % 2) + (me // 4 + at) % 4
    table = jnp.where(at == STRIPS, me % 4, table).astype(jnp.int32)

    picked = jnp.sum(jnp.where(jnp.arange(groups) == group, exps, 0))
    scale_up = jnp.left_shift(1, picked).astype(jnp.float32)
    delta = params - local_params[0].astype(jnp.float32)
    coded = jnp.clip(delta * scale_up, -448.0, 448.0).astype(jnp.bfloat16)
    total = lax.psum(coded.astype(jnp.float32) / scale_up, "rep")

    half = B // 2
    b_low, b_high, c_low = A, A + half, A + B
    a, turned = all_products(inputs, cotangent, table, A)
    a_x = over_x(a).reshape(2, 4, A, WIDTH)
    b_far = products(
        inputs,
        turned,
        table,
        2,
        lambda i: 2 + 4 * i,
        [(b_low, half, 0, 2, 1, 1), (b_high, half, 0, 2, 1, 1)],
        [a],
    )
    b_up1, b_down1 = along("y", b_far[0], 1), along("y", b_far[1], -1)
    c_far = crossing_products(inputs, turned, table, c_low, C // 2, b_far[:1])
    c_z = [along_z(array) for array in c_far]
    c_places = {(2, 0): (0, 0), (2, 1): (0, 1), (1, 1): (0, 2), (3, 0): (0, 3)}
    c_places |= {(1, 0): (1, 0), (3, 1): (1, 1), (0, 0): (2, 0), (0, 1): (2, 1)}
    b_near = products(
        inputs,
        turned,
        table,
        4,
        lambda i: 1 + 4 * lax.rem(i, 2) + 2 * (i // 2),
        [(low, half, first, 2, 1, 1) for first in (0, 2) for low in (b_low, b_high)],
        c_far[:1],
    )
    b_up2, b_down2 = along("y", b_near[1], 1), along("y", b_near[2], -1)
    *b_own, c_near = products(
        inputs,
        turned,
        table,
        5,
        lambda i: jnp.where(i == 0, 4, i - 1),
        [(b_low, half, 0, 2, -1, 1), (b_high, half, 0, 2, -1, 1), (c_low, C, 1, 4, 1, 0)],
        b_near[:1],
    )

    def b_third(near_up, near_down, got_up, got_down, up, down):
        up[...] = near_up[...] + got_up[...]
        down[...] = near_down[...] + got_down[...]

    b_last = combine(b_third, [b_near[0], b_near[3], b_up1, b_down1], [(2, ROW, half, WIDTH)] * 2, [c_near])
    b_up3, b_down3 = along("y", b_last[0], 1), along("y", b_last[1], -1)

    def b_terms(dx, h):
        arrays = (b_own[0], b_down2, b_up3) if h == 0 else (b_own[1], b_up2, b_down3)
        return [(array, (2, 1, half, WIDTH), (0, dx, 0, 0)) for array in arrays]

    def c_terms(dy, h):
        block = (1, ROW, C // 2, WIDTH)
        array, n = c_places[dy, h]
        return [(c_near, block, (dy, 0, h, 0)), (c_z[array], block, (n, 0, 0, 0))]

    def a_terms(dy, h):
        return [(a_x, (2, 1, A // 2, WIDTH), (0, dy, h, 0))]

    def whole(arrived):
        return [
            (array, array.shape, (0,) * 3) if n is None else (array, (1,) + array.shape[1:], (n, 0, 0, 0))
            for array, n in arrived
        ]

    def nesterov(weights, moment, total, new_weights, fresh):
        outer_grad = total[...] / groups
        fresh[...] = 0.9 * moment[...] + outer_grad
        new_weights[...] = weights[...] - 0.7 * (outer_grad + 0.9 * fresh[...])

    new_params, new_momentum = combine(nesterov, [params, momentum, total], [params.shape] * 2, b_last[:1])

    ring_b = reduce_ring("x", b_terms, 2, half)
    ring_c = reduce_ring("y", c_terms, ROW, C // 2)
    ring_a = reduce_ring("y", a_terms, 2, A // 2)
    next(ring_b), next(ring_c), next(ring_a)
    done = ring_c.send([new_params])
    done = ring_b.send(done)
    done, c_got = ring_c.send(done)
    done = ring_a.send(done)
    done, b_got = ring_b.send(done)

    def keep_and_cross(low, high, keep, cross):
        rows = low.shape[1]
        keep[:rows, :], keep[rows:, :] = low[0], high[0]
        cross[:rows, :], cross[rows:, :] = low[1], high[1]

    def c_home(low, high, out):
        out[:, : C // 2, :], out[:, C // 2 :, :] = low, high

    (c_sum,) = settle(
        c_terms(0, 0) + whole(c_got(0)), c_terms(0, 1) + whole(c_got(1)), c_home, [(ROW, C, WIDTH)], done
    )
    c_own = over_x(c_sum)
    b_keep, b_cross = settle(
        b_terms(0, 0) + whole(b_got(0)), b_terms(0, 1) + whole(b_got(1)), keep_and_cross, [(B, WIDTH)] * 2, [c_sum]
    )
    b_in = along_z(b_cross)
    done, a_got = ring_a.send([b_keep])

    a_keep, a_cross = settle(
        a_terms(0, 0) + whole(a_got(0)), a_terms(0, 1) + whole(a_got(1)), keep_and_cross, [(A, WIDTH)] * 2, done + [b_in]
    )
    a_in = along_z(a_cross)

    def assemble(keep_a, got_a, keep_b, got_b, own_c, out):
        value = jnp.concatenate([keep_a[...] + got_a[...], keep_b[...] + got_b[...], own_c[...]], axis=0)
        out[0] = value.T

    (kv_grad,) = combine(
        assemble, [a_keep, a_in, b_keep, b_in, c_own], [(1, WIDTH, A + B + C)]
    )
    return (new_params, new_momentum, kv_grad)


def solution(mesh):
    in_specs = (
        P("fsdp", None),
        P("fsdp", None),
        P("rep", "fsdp", None),
        P(),
        P(("rep", "fsdp"), None),
        P(("rep", "fsdp"), None),
    )
    out_specs = (P("fsdp", None), P("fsdp", None), P("rep", "fsdp", None))
    return jax.shard_map(local, mesh=mesh, in_specs=in_specs, out_specs=out_specs, check_vma=False)
```

```python
import jax
import jax.numpy as jnp
from jax import lax
from jax.experimental import pallas as pl
from jax.experimental.pallas import tpu as pltpu
from jax.sharding import PartitionSpec as P

WIDTH = 256
ROW = 4
STRIP = ROW * WIDTH
STRIPS = 8
A = 384
B = 320
C = 320
X_RINGS = [[16 * z + 4 * y + x for x in range(4)] for z in range(2) for y in range(4)]
LONG = pl.CostEstimate(flops=2 * 10**10, bytes_accessed=1000, transcendentals=0)
SHORT = pl.CostEstimate(flops=4 * 10**9, bytes_accessed=1000, transcendentals=0)
MIB = 1024 * 1024


def all_products(inputs, cotangent, table, height):
    depth, columns = cotangent.shape

    def body(table, x, k, out, turned):
        step = pl.program_id(0)

        @pl.when(step == 0)
        def _():
            turned[...] = k[...].T

        value = jnp.dot(turned[:height, :], x[...], preferred_element_type=jnp.float32)
        for place in range(ROW):
            out[place, 0] = value[:, place * WIDTH : (place + 1) * WIDTH]

    out, turned = pl.pallas_call(
        body,
        grid_spec=pltpu.PrefetchScalarGridSpec(
            num_scalar_prefetch=1,
            grid=(STRIPS,),
            in_specs=[
                pl.BlockSpec((depth, STRIP), lambda i, table: (0, table[i])),
                pl.BlockSpec((depth, columns), lambda i, table: (0, 0), pipeline_mode=pl.Buffered(1)),
            ],
            out_specs=[
                pl.BlockSpec((ROW, 1, height, WIDTH), lambda i, table: (0, i, 0, 0)),
                pl.BlockSpec(memory_space=pltpu.VMEM),
            ],
        ),
        out_shape=[
            jax.ShapeDtypeStruct((ROW, STRIPS, height, WIDTH), jnp.float32),
            pltpu.VMEM((columns, depth), cotangent.dtype),
        ],
        compiler_params=pltpu.CompilerParams(dimension_semantics=("arbitrary",), vmem_limit_bytes=60 * MIB),
        cost_estimate=LONG,
    )(table, inputs, cotangent)
    return out, pltpu.with_memory_space_constraint(turned, pltpu.VMEM)


def crossing_products(inputs, turned, table, low, half, after):
    depth = inputs.shape[0]

    def body(table, x, k, *refs):
        soon, later, last = refs[-3:]
        step = pl.program_id(0)

        def emit(h, out, n):
            value = jnp.dot(k[low + h * half : low + (h + 1) * half, :], x[...], preferred_element_type=jnp.float32)
            for place in range(ROW):
                out[n, (place - table[STRIPS]) & (ROW - 1)] = value[:, place * WIDTH : (place + 1) * WIDTH]

        for at, first, second in ((0, soon, soon), (1, later, soon), (2, soon, later), (3, last, last)):

            @pl.when(step == at)
            def _(at=at, first=first, second=second):
                emit(0, first, 1 if at == 2 else 0)
                emit(1, second, 0 if at == 1 else 1)

    block = (2, ROW, half, WIDTH)
    return pl.pallas_call(
        body,
        grid_spec=pltpu.PrefetchScalarGridSpec(
            num_scalar_prefetch=1,
            grid=(4,),
            in_specs=[
                pl.BlockSpec(
                    (depth, STRIP),
                    lambda i, table: (0, table[4 + jnp.where(i == 0, 2, jnp.where(i == 3, 0, 2 * i - 1))]),
                ),
                pl.BlockSpec(memory_space=pltpu.VMEM),
            ]
            + [pl.BlockSpec(memory_space=pl.ANY)] * len(after),
            out_specs=[
                pl.BlockSpec(block, lambda i, table: (jnp.minimum(i, 1), 0, 0, 0)),
                pl.BlockSpec(block, lambda i, table: (0, 0, 0, 0)),
                pl.BlockSpec(block, lambda i, table: (0, 0, 0, 0)),
            ],
        ),
        out_shape=[jax.ShapeDtypeStruct((n, ROW, half, WIDTH), jnp.float32) for n in (4, 2, 2)],
        compiler_params=pltpu.CompilerParams(dimension_semantics=("arbitrary",), vmem_limit_bytes=60 * MIB),
        cost_estimate=LONG,
    )(table, inputs, turned, *after)


def products(inputs, turned, table, count, strip_of, wanted, after):
    depth = inputs.shape[0]

    def body(table, x, k, *refs):
        outs = refs[len(after) :]
        step = pl.program_id(0)
        for (low, height, first, number, _), out in zip(wanted, outs):

            def emit(low=low, height=height, out=out):
                value = jnp.dot(k[low : low + height, :], x[...], preferred_element_type=jnp.float32)
                for place in range(ROW):
                    out[0, (place - table[STRIPS]) & (ROW - 1)] = value[:, place * WIDTH : (place + 1) * WIDTH]

            if number == count:
                emit()
            else:
                pl.when((step >= first) & (step < first + number))(emit)

    def out_spec(low, height, first, number, order):
        def at(i, table):
            n = jnp.clip(i - first, 0, number - 1)
            return (n if order > 0 else number - 1 - n, 0, 0, 0)

        return pl.BlockSpec((1, ROW, height, WIDTH), at)

    return pl.pallas_call(
        body,
        grid_spec=pltpu.PrefetchScalarGridSpec(
            num_scalar_prefetch=1,
            grid=(count,),
            in_specs=[
                pl.BlockSpec((depth, STRIP), lambda i, table: (0, table[strip_of(i)])),
                pl.BlockSpec(memory_space=pltpu.VMEM),
            ]
            + [pl.BlockSpec(memory_space=pl.ANY)] * len(after),
            out_specs=[out_spec(*w) for w in wanted],
        ),
        out_shape=[jax.ShapeDtypeStruct((w[3], ROW, w[1], WIDTH), jnp.float32) for w in wanted],
        compiler_params=pltpu.CompilerParams(dimension_semantics=("arbitrary",), vmem_limit_bytes=60 * MIB),
        cost_estimate=LONG,
    )(table, inputs, turned, *after)


def combine(body, pieces, shapes, after=()):
    pieces = [p if isinstance(p, tuple) else (p, p.shape, (0,) * p.ndim) for p in pieces]

    def kernel(*refs):
        body(*refs[: len(pieces)], *refs[len(pieces) + len(after) :])

    return pl.pallas_call(
        kernel,
        grid=(1,),
        in_specs=[pl.BlockSpec(block, lambda i, at=at: at) for _, block, at in pieces]
        + [pl.BlockSpec(memory_space=pl.ANY)] * len(after),
        out_specs=[pl.BlockSpec(s, lambda i, at=(0,) * len(s): at) for s in shapes],
        out_shape=[jax.ShapeDtypeStruct(s, jnp.float32) for s in shapes],
        compiler_params=pltpu.CompilerParams(vmem_limit_bytes=60 * MIB),
        cost_estimate=SHORT,
    )(*[p[0] for p in pieces], *after)


def along(axis, array, step):
    stride = 1 if axis == "x" else 4
    pairs = [(f, f + ((f // stride + step) % 4 - f // stride % 4) * stride) for f in range(32)]
    return lax.ppermute(array, "fsdp", pairs)


def along_z(array):
    return lax.ppermute(array, "fsdp", [(f, (f + 16) % 32) for f in range(32)])


def over_x(array):
    return lax.psum_scatter(array, "fsdp", scatter_dimension=0, axis_index_groups=X_RINGS, tiled=True)[0]


def reduce_ring(axis, terms, outer, rows):
    shape = (outer, rows, WIDTH)
    count = len(terms(0, 0))

    def total(refs):
        value = refs[0][...].reshape(shape)
        for ref in refs[1:]:
            value = value + ref[...].reshape(shape)
        return value

    def first(*refs):
        up, down = refs[4 * count :]
        up[0], up[1], down[0], down[1] = [total(refs[i * count : (i + 1) * count]) for i in range(4)]

    after = yield
    pieces = terms(2, 0) + terms(1, 1) + terms(2, 1) + terms(3, 0)
    up, down = combine(first, pieces, [(2,) + shape] * 2, after)
    up_in, down_in = along(axis, up, 1), along(axis, down, -1)
    after = yield [up]

    def got(array):
        return [(array, (1,) + shape, (0, 0, 0, 0))]

    def second(*refs):
        up, down = refs[-2:]
        up[...], down[...] = total(refs[: count + 1]), total(refs[count + 1 : -2])

    pieces = terms(1, 0) + got(up_in) + terms(3, 1) + got(down_in)
    up, down = combine(second, pieces, [shape] * 2, after)
    up_last, down_last = along(axis, up, 1), along(axis, down, -1)
    yield [up], lambda half: [(down_in, 1), (up_last, None)] if half == 0 else [(up_in, 1), (down_last, None)]


def settle(low, high, write, shapes, after):
    def body(*refs):
        sums = []
        for group, pieces in ((refs[: len(low)], low), (refs[len(low) : len(low) + len(high)], high)):
            shape = [n for n in pieces[-1][1]]
            value = group[0][...].reshape(shape)
            for ref in group[1:]:
                value = value + ref[...].reshape(shape)
            sums.append(value)
        write(*sums, *refs[len(low) + len(high) :])

    return combine(body, low + high, shapes, after)


def local(params, momentum, local_params, exps, inputs, cotangent):
    groups = lax.axis_size("rep")
    group = lax.axis_index("rep")
    me = lax.axis_index("fsdp")
    at = jnp.arange(STRIPS + 1)
    table = 4 * ((me // 16 + at // 4) % 2) + (me // 4 + at) % 4
    table = jnp.where(at == STRIPS, me % 4, table).astype(jnp.int32)

    picked = lax.dynamic_index_in_dim(exps, group, keepdims=False)
    scale_up = jnp.left_shift(1, picked).astype(jnp.float32)
    delta = params - local_params[0].astype(jnp.float32)
    coded = jnp.clip(delta * scale_up, -448.0, 448.0).astype(jnp.bfloat16)
    total = lax.psum(coded.astype(jnp.float32) / scale_up, "rep")

    half = B // 2
    b_low, b_high, c_low = A, A + half, A + B
    a, turned = all_products(inputs, cotangent, table, A)
    a_x = over_x(a).reshape(2, 4, A, WIDTH)
    b_far = products(
        inputs,
        turned,
        table,
        2,
        lambda i: 2 + 4 * i,
        [(b_low, half, 0, 2, 1), (b_high, half, 0, 2, 1)],
        [a],
    )
    b_up1, b_down1 = along("y", b_far[0], 1), along("y", b_far[1], -1)
    c_far = crossing_products(inputs, turned, table, c_low, C // 2, b_far[:1])
    c_z = [along_z(array) for array in c_far]
    c_places = {(2, 0): (0, 0), (2, 1): (0, 1), (1, 1): (0, 2), (3, 0): (0, 3)}
    c_places |= {(1, 0): (1, 0), (3, 1): (1, 1), (0, 0): (2, 0), (0, 1): (2, 1)}
    b_near = products(
        inputs,
        turned,
        table,
        4,
        lambda i: 1 + 4 * lax.rem(i, 2) + 2 * (i // 2),
        [(low, half, first, 2, 1) for first in (0, 2) for low in (b_low, b_high)],
        c_far[:1],
    )
    b_up2, b_down2 = along("y", b_near[1], 1), along("y", b_near[2], -1)
    *b_own, c_near = products(
        inputs,
        turned,
        table,
        5,
        lambda i: jnp.where(i == 0, 4, i - 1),
        [(b_low, half, 0, 2, -1), (b_high, half, 0, 2, -1), (c_low, C, 1, 4, 1)],
        b_near[:1],
    )

    def b_third(near_up, near_down, got_up, got_down, up, down):
        up[...] = near_up[...] + got_up[...]
        down[...] = near_down[...] + got_down[...]

    b_last = combine(b_third, [b_near[0], b_near[3], b_up1, b_down1], [(2, ROW, half, WIDTH)] * 2, [c_near])
    b_up3, b_down3 = along("y", b_last[0], 1), along("y", b_last[1], -1)

    def b_terms(dx, h):
        arrays = (b_own[0], b_down2, b_up3) if h == 0 else (b_own[1], b_up2, b_down3)
        return [(array, (2, 1, half, WIDTH), (0, dx, 0, 0)) for array in arrays]

    def c_terms(dy, h):
        block = (1, ROW, C // 2, WIDTH)
        array, n = c_places[dy, h]
        return [(c_near, block, (dy, 0, h, 0)), (c_z[array], block, (n, 0, 0, 0))]

    def a_terms(dy, h):
        return [(a_x, (2, 1, A // 2, WIDTH), (0, dy, h, 0))]

    def whole(arrived):
        return [
            (array, array.shape, (0,) * 3) if n is None else (array, (1,) + array.shape[1:], (n, 0, 0, 0))
            for array, n in arrived
        ]

    def nesterov(weights, moment, total, new_weights, fresh):
        outer_grad = total[...] / groups
        fresh[...] = 0.9 * moment[...] + outer_grad
        new_weights[...] = weights[...] - 0.7 * (outer_grad + 0.9 * fresh[...])

    new_params, new_momentum = combine(nesterov, [params, momentum, total], [params.shape] * 2, b_last[:1])

    ring_b = reduce_ring("x", b_terms, 2, half)
    ring_c = reduce_ring("y", c_terms, ROW, C // 2)
    ring_a = reduce_ring("y", a_terms, 2, A // 2)
    next(ring_b), next(ring_c), next(ring_a)
    done = ring_c.send([new_params])
    done = ring_b.send(done)
    done, c_got = ring_c.send(done)
    done = ring_a.send(done)
    done, b_got = ring_b.send(done)

    def c_x_terms(dx, h):
        block = (1, 1, C // 2, WIDTH)
        terms = [(c_near, block, (0, dx, h, 0)), (c_z[2], block, (h, dx, 0, 0))]
        for array, n in c_got(h):
            terms.append((array, block[1:], (dx, 0, 0)) if n is None else (array, block, (n, dx, 0, 0)))
        return terms

    def keep_and_cross(low, high, keep, cross):
        rows = low.shape[1]
        keep[:rows, :], keep[rows:, :] = low[0], high[0]
        cross[:rows, :], cross[rows:, :] = low[1], high[1]

    ring_cx = reduce_ring("x", c_x_terms, 1, C // 2)
    next(ring_cx)
    done = ring_cx.send(done)
    b_keep, b_cross = settle(
        b_terms(0, 0) + whole(b_got(0)), b_terms(0, 1) + whole(b_got(1)), keep_and_cross, [(B, WIDTH)] * 2, done
    )
    b_in = along_z(b_cross)
    done, cx_got = ring_cx.send([b_keep])
    done, a_got = ring_a.send(done)

    def c_home(low, high, out):
        out[: C // 2, :], out[C // 2 :, :] = low[0], high[0]

    (c_own,) = settle(
        c_x_terms(0, 0) + whole(cx_got(0)), c_x_terms(0, 1) + whole(cx_got(1)), c_home, [(C, WIDTH)], done
    )
    a_keep, a_cross = settle(
        a_terms(0, 0) + whole(a_got(0)), a_terms(0, 1) + whole(a_got(1)), keep_and_cross, [(A, WIDTH)] * 2, [c_own, b_in]
    )
    a_in = along_z(a_cross)

    def assemble(keep_a, got_a, keep_b, got_b, own_c, out):
        value = jnp.concatenate([keep_a[...] + got_a[...], keep_b[...] + got_b[...], own_c[...]], axis=0)
        out[0] = value.T

    (kv_grad,) = combine(
        assemble, [a_keep, a_in, b_keep, b_in, c_own], [(1, WIDTH, A + B + C)]
    )
    return (new_params, new_momentum, kv_grad)


def solution(mesh):
    in_specs = (
        P("fsdp", None),
        P("fsdp", None),
        P("rep", "fsdp", None),
        P(),
        P(("rep", "fsdp"), None),
        P(("rep", "fsdp"), None),
    )
    out_specs = (P("fsdp", None), P("fsdp", None), P("rep", "fsdp", None))
    return jax.shard_map(local, mesh=mesh, in_specs=in_specs, out_specs=out_specs, check_vma=False)
```
